256 devices in a mesh: freq: 8 (over x, z_lo), space: 32 (over z_hi, y, core).
Axes of the slice: x: 4, y: 4, z: 8 (z_hi: 4, z_lo: 2; z = z_hi * 2 + z_lo), core: 2. Of those that a mesh axis runs over, the one named last changes fastest.
Arguments:
- wavefield: float32 [8, 2, 2048, 4096], P('freq', None, 'space'), may hold values from -6 to 6
- velocity: float32 [8, 2048, 4096], P('freq', 'space'), may hold values from 1500 to 4500
- freq_index: int32 [8], P('freq'), may hold values from 0 to 63
- owner: int32 [8], replicated, may hold values from 0 to 7, each once
Outputs:
- image: float32 [2, 2048, 4096], P(None, 'space', 'freq')
- final_field: float32 [8, 2, 2048, 4096], P('freq', None, 'space')
The draws below stay inside these ranges and needn't reach their ends.
Inputs may be any that keep to these rules, and one draw needn't show every extreme that they name: `owner`: each stored slice number appears once.
All inputs are finite; a program needn't handle non-finite values.
Results may differ from the reference program's by a relative error of at most 0.00022.
Values sent between devices are 32-bit elements; how exact they have to be, the bound alone decides.
A program may use at most 128 MiB of HBM per device.

```python
import math
import jax
import jax.numpy as jnp

NX = 4096
NY = 2048
STEPS = 2
NFREQ = 8
SLICES = 8


def place_ends(array, own_key, smallest, high):
    dims = array.shape
    index_at = [jax.random.randint(jax.random.fold_in(own_key, axis), (), 0, dims[axis]) for axis in range(len(dims))]
    array = array.at[tuple(index_at)].set(smallest)
    longest = dims.index(max(dims))
    index_at[longest] = (index_at[longest] + 1) % dims[longest]
    return array.at[tuple(index_at)].set(high)


def steps_of(stream_key, extent, split, low, top_value):
    def one(axis_at, parts):
        draws = jax.random.uniform(jax.random.fold_in(jax.random.fold_in(stream_key, 6), axis_at), (parts,), jnp.float32, low / len(split), top_value / len(split))
        return jnp.repeat(jnp.exp(draws), extent[axis_at] // parts).reshape((-1,) + (1,) * (len(extent) - axis_at - 1))

    gain = one(*split[0])
    for cut in split[1:]:
        gain = gain * one(*cut)
    return gain


def scatter_about(own_key, extent, spread, bound, split=(), kind=jnp.bfloat16):
    entries = spread * jax.random.normal(own_key, extent, jnp.float32)
    if split:
        entries = entries * steps_of(own_key, extent, split, -0.22, 0.18)
    return jnp.clip(entries, -bound, bound).astype(kind)


def setup_inputs(seed: int = 0) -> dict:
    arg_keys = jax.random.split(jax.random.key(seed), 5)
    return {
        "wavefield": scatter_about(arg_keys[0], (NFREQ, 2, NY, NX), 1.0, 6.0, ((0, 8), (2, 32)), jnp.float32),
        "velocity": jnp.clip(jnp.exp(math.log(4500.0) - 1.0986123 * jax.random.uniform(arg_keys[1], (SLICES, NY, NX), jnp.float32) ** steps_of(arg_keys[1], (SLICES, NY, NX), ((0, 8), (1, 32)), -0.2, 0.2)), 1500.0, 4500.0),
        "freq_index": place_ends(jax.random.randint(arg_keys[2], (NFREQ,), 0, 64), jax.random.fold_in(arg_keys[2], 1), 0, 63).astype(jnp.int32),
        "owner": jax.random.permutation(arg_keys[3], SLICES).astype(jnp.int32),
    }


cell_spacing = 25.0
layer_thickness = 10.0
base_speed = 1500.0
lowest_hertz = 5.0
hertz_step = 0.9

def reference(wavefield, velocity, freq_index, owner):
    kx_vals = jnp.fft.fftfreq(NX, d=cell_spacing) * (2 * math.pi)
    ky_vals = jnp.fft.fftfreq(NY, d=cell_spacing) * (2 * math.pi)
    wave_sq = ky_vals[:, None] ** 2 + kx_vals[None, :] ** 2
    omega = 2 * math.pi * (lowest_hertz + hertz_step * freq_index.astype(jnp.float32))
    fields = [wavefield[slot, 0] + 1j * wavefield[slot, 1] for slot in range(NFREQ)]
    images = []
    for depth in range(STEPS):
        speed = velocity[owner[depth]]
        slowness = 1.0 / speed - 1.0 / base_speed
        total = jnp.zeros((NY, NX), dtype=wavefield.dtype)
        for slot in range(NFREQ):
            vertical = (omega[slot] / base_speed) ** 2 - wave_sq
            damping = jnp.exp(-layer_thickness * jnp.sqrt(jnp.maximum(-vertical, 0.0)))
            angle = layer_thickness * jnp.sqrt(jnp.maximum(vertical, 0.0))
            spectrum = jnp.fft.fft2(fields[slot])
            spectrum = spectrum * (damping * jnp.cos(angle) + 1j * damping * jnp.sin(angle))
            field = jnp.fft.ifft2(spectrum)
            shift = omega[slot] * layer_thickness * slowness
            field = field * (jnp.cos(shift) + 1j * jnp.sin(shift))
            fields[slot] = field
            total = total + field.real
        images.append(total)
    final_field = jnp.stack([jnp.stack([item.real, item.imag], axis=0) for item in fields], axis=0)
    return (jnp.stack(images, axis=0), final_field)
```

```python
import functools
import math

import jax
import jax.numpy as jnp
import ml_dtypes
import numpy as np
from jax import lax
from jax.experimental import pallas as pl
from jax.experimental.pallas import tpu as pltpu
from jax.sharding import PartitionSpec as P

NX, NY = 4096, 2048
SPACE, FREQ = 32, 8
ROWS = NY // SPACE
LANES = 128
TILES = NX // LANES
YA = NY // LANES
CHUNK = 32
CHUNKS = ROWS // CHUNK
BAND = NX // FREQ
PIECE = ROWS // FREQ

cell_spacing = 25.0
layer_thickness = 10.0
base_speed = 1500.0
lowest_hertz = 5.0
hertz_step = 0.9
MESH = pl.DeviceIdType.MESH
f32 = jnp.float32
bf16 = jnp.bfloat16


def times_root(value, power, length, sign):
    re, im = value
    power = power % length
    quarter = 4 * power
    if quarter % length == 0:
        turn = quarter // length
        if sign < 0:
            turn = (4 - turn) % 4
        return [(re, im), (-im, re), (-re, -im), (im, -re)][turn]
    angle = sign * 2 * math.pi * power / length
    c, s = math.cos(angle), math.sin(angle)
    if (8 * power) % length == 0:
        h = math.sqrt(0.5)
        cs, ss = math.copysign(1, c), math.copysign(1, s)
        p, q = re * h, im * h
        real = (p if cs > 0 else -p) + (-q if ss > 0 else q)
        imag = (p if ss > 0 else -p) + (q if cs > 0 else -q)
        return (real, imag)
    return (re * c - im * s, re * s + im * c)


def add(a, b):
    return (a[0] + b[0], a[1] + b[1])


def sub(a, b):
    return (a[0] - b[0], a[1] - b[1])


def small_dft(values, sign):
    n = len(values)
    if n == 1:
        return values
    if n == 2:
        return [add(values[0], values[1]), sub(values[0], values[1])]
    m = n // 4
    parts = [small_dft(values[r::4], sign) for r in range(4)]
    out = [None] * n
    for k in range(m):
        a = parts[0][k]
        b, c, d = (times_root(parts[r][k], r * k, n, sign) for r in (1, 2, 3))
        s0, s1 = add(a, c), sub(a, c)
        s2, s3 = add(b, d), times_root(sub(b, d), 1, 4, sign)
        out[k], out[k + m] = add(s0, s2), add(s1, s3)
        out[k + 2 * m], out[k + 3 * m] = sub(s0, s2), sub(s1, s3)
    return out


def sin_cos(t):
    n = jnp.floor(t * (2 / math.pi) + 0.5)
    r = (t - n * 1.5703125) - n * 4.83826794896e-4
    z = r * r
    s = r + r * z * (-1.6666654611e-1 + z * (8.3321608736e-3 + z * -1.9515295891e-4))
    c = 1.0 - 0.5 * z + z * z * (4.166664568298827e-2 + z * (-1.388731625493765e-3 + z * 2.443315711809948e-5))
    half = n * 0.5
    odd = half != jnp.floor(half)
    quad = n - 4.0 * jnp.floor(n * 0.25)
    sine = jnp.where(odd, c, s)
    cosine = jnp.where(odd, s, c)
    sine = jnp.where(quad >= 2.0, -sine, sine)
    cosine = jnp.where((quad == 1.0) | (quad == 2.0), -cosine, cosine)
    return sine, cosine


def split(value):
    high = value.astype(bf16)
    return high, (value - high.astype(f32)).astype(bf16)


def mul3(a, b):
    ah, al = a
    bh, bl = b
    dot = functools.partial(jnp.dot, preferred_element_type=f32)
    return dot(ah, bh) + (dot(al, bh) + dot(ah, bl))


def kernel(
    fidx_ref, owner_ref, wave_ref, vel_ref, txc_ref, txs_ref, rh_ref, rl_ref, lh_ref, ll_ref,
    image_ref, field_ref,
    rowbuf, sendx, sendy, recvy, recvx, mid, hcos, hsin, tyc, tys,
    vrecv, vsel, slow, phc, phs, terms, imag, irecv,
    asend, arecv, aloc, vsend, vrcv, vloc, gsend, grecv, isend, ircv, iloc,
):
    f = lax.axis_index("freq")
    me = lax.axis_index("space")
    zh, yy, cc = me // 8, (me // 2) % 4, me % 2

    def space_peer(j):
        return ((zh + j // 8) % 4 * 4 + (yy + (j // 2) % 4) % 4) * 2 + (cc + j % 2) % 2

    def freq_peer(j):
        return (f + j) % FREQ

    barrier = pltpu.get_barrier_semaphore()

    @pl.loop(1, SPACE)
    def _(j):
        pl.semaphore_signal(barrier, inc=1, device_id=(f, space_peer(j)), device_id_type=MESH)

    @pl.loop(1, FREQ)
    def _(j):
        pl.semaphore_signal(barrier, inc=1, device_id=(freq_peer(j), me), device_id_type=MESH)

    pl.semaphore_wait(barrier, SPACE + FREQ - 2)

    def remote(src, dst, send, recv, device):
        return pltpu.make_async_remote_copy(
            src_ref=src, dst_ref=dst, send_sem=send, recv_sem=recv, device_id=device, device_id_type=MESH
        )

    def a2a_start(src, dst, ch, i):
        rows = pl.ds(ch * CHUNK, CHUNK)

        @pl.loop(1, SPACE)
        def _(j):
            d = space_peer(j)
            remote(src.at[d, rows], dst.at[me, rows], asend.at[i, ch], arecv.at[i, ch], (f, d)).start()

        pltpu.make_async_copy(src.at[me, rows], dst.at[me, rows], aloc.at[i, ch]).start()

    def a2a_all(src, dst, ch, i):
        rows = pl.ds(ch * CHUNK, CHUNK)
        some = pl.ds(0, SPACE - 1)
        return remote(src.at[some, rows], dst.at[some, rows], asend.at[i, ch], arecv.at[i, ch], (f, me))

    def a2a_wait_recv(src, dst, ch, i):
        rows = pl.ds(ch * CHUNK, CHUNK)
        a2a_all(src, dst, ch, i).wait_recv()
        pltpu.make_async_copy(src.at[me, rows], dst.at[me, rows], aloc.at[i, ch]).wait()

    def forward_x(re_ref, im_ref, dst, ch):
        @pl.loop(0, CHUNK // 8)
        def _(g):
            rows = pl.ds(pl.multiple_of(ch * CHUNK + g * 8, 8), 8)
            local = pl.ds(pl.multiple_of(g * 8, 8), 8)
            vals = [
                (re_ref[rows, a * LANES:(a + 1) * LANES], im_ref[rows, a * LANES:(a + 1) * LANES])
                for a in range(TILES)
            ]
            vals = small_dft(vals, -1)
            for k in range(TILES):
                re, im = vals[k]
                c, s = txc_ref[k:k + 1, :], txs_ref[k:k + 1, :]
                rowbuf[k, local, 0:LANES] = re * c + im * s
                rowbuf[k, local, LANES:] = im * c - re * s

        @pl.loop(0, TILES // 8)
        def _(g):
            some = pl.ds(g * 8, 8)
            block = rowbuf[some].reshape(8 * CHUNK, 2 * LANES)
            out = mul3(split(block), (rh_ref[...], rl_ref[...]))
            dst[some, pl.ds(ch * CHUNK, CHUNK), :] = out.reshape(8, CHUNK, 2 * LANES)

    def inverse_x(src, step, re_ref, im_ref, ch):
        @pl.loop(0, TILES // 8)
        def _(g):
            some = pl.ds(g * 8, 8)
            block = src[some, pl.ds(ch * CHUNK, CHUNK), :].reshape(8 * CHUNK, 2 * LANES)
            out = mul3(split(block), (lh_ref[...], ll_ref[...]))
            rowbuf[some] = out.reshape(8, CHUNK, 2 * LANES)

        @pl.loop(0, CHUNK // 8)
        def _(g):
            rows = pl.ds(pl.multiple_of(ch * CHUNK + g * 8, 8), 8)
            local = pl.ds(pl.multiple_of(g * 8, 8), 8)
            vals = []
            for k in range(TILES):
                re, im = rowbuf[k, local, 0:LANES], rowbuf[k, local, LANES:]
                c, s = txc_ref[k:k + 1, :], txs_ref[k:k + 1, :]
                vals.append((re * c - im * s, im * c + re * s))
            vals = small_dft(vals, 1)
            for a in range(TILES):
                re, im = vals[a]
                cols = slice(a * LANES, (a + 1) * LANES)
                c, s = phc[step, rows, cols], phs[step, rows, cols]
                re_ref[rows, cols] = re * c - im * s
                im_ref[rows, cols] = re * s + im * c

    def column_pass(src, dst, i):
        @pl.loop(0, LANES // 8)
        def _(t):
            half, sub_rows = t // 8, pl.ds(pl.multiple_of(t % 8 * 8, 8), 8)
            vals = [
                (src[2 * a + half, sub_rows, 0:LANES], src[2 * a + half, sub_rows, LANES:]) for a in range(YA)
            ]
            vals = small_dft(vals, -1)
            re_rows = pl.ds(pl.multiple_of(t * 8, 8), 8)
            im_rows = pl.ds(pl.multiple_of(LANES + t * 8, 8), 8)
            for k in range(YA):
                re, im = vals[k]
                cols = slice(k % 2 * LANES, k % 2 * LANES + LANES)
                c, s = tyc[k // 2, re_rows, cols], tys[k // 2, re_rows, cols]
                mid[k // 2, re_rows, cols] = re * c + im * s
                mid[k // 2, im_rows, cols] = im * c - re * s

        @pl.loop(0, YA // 2)
        def _(k):
            left = (lh_ref[...], ll_ref[...])
            spec = mul3(left, split(mid[k]))
            re, im = spec[:LANES], spec[LANES:]
            c, s = hcos[k], hsin[k]
            spec = jnp.concatenate([re * c - im * s, re * s + im * c], axis=0)
            mid[k] = mul3((rh_ref[...], rl_ref[...]), split(spec))

        for ch in range(CHUNKS):
            @pl.loop(0, CHUNK // 4)
            def _(q):
                half, tile = q % 2, ch * (CHUNK // 8) + q // 2
                t = half * 8 + tile
                re_rows = pl.ds(pl.multiple_of(t * 8, 8), 8)
                im_rows = pl.ds(pl.multiple_of(LANES + t * 8, 8), 8)
                vals = []
                for k in range(YA):
                    cols = slice(k % 2 * LANES, k % 2 * LANES + LANES)
                    re, im = mid[k // 2, re_rows, cols], mid[k // 2, im_rows, cols]
                    c, s = tyc[k // 2, re_rows, cols], tys[k // 2, re_rows, cols]
                    vals.append((re * c - im * s, im * c + re * s))
                vals = small_dft(vals, 1)
                out_rows = pl.ds(pl.multiple_of(tile * 8, 8), 8)
                for a in range(YA):
                    dst[2 * a + half, out_rows, 0:LANES] = vals[a][0]
                    dst[2 * a + half, out_rows, LANES:] = vals[a][1]
            a2a_start(dst, recvx.at[i // 2], ch, i)

    omega = 2 * math.pi * (lowest_hertz + hertz_step * fidx_ref[0].astype(f32))

    def make_tables():
        kb = lax.broadcasted_iota(jnp.int32, (LANES, LANES), 0)
        lane = lax.broadcasted_iota(jnp.int32, (LANES, LANES), 1)
        jx = me + TILES * lane
        kx = jnp.where(jx < NX // 2, jx, jx - NX).astype(f32) * (2 * math.pi / (NX * cell_spacing))

        @pl.loop(0, YA // 2)
        def _(k):
            for part in range(2):
                ka = 2 * k + part
                cols = slice(part * LANES, (part + 1) * LANES)
                jy = ka + YA * kb
                ky = jnp.where(jy < NY // 2, jy, jy - NY).astype(f32) * (2 * math.pi / (NY * cell_spacing))
                vertical = (omega / base_speed) ** 2 - (ky * ky + kx * kx)
                root = layer_thickness * jnp.sqrt(jnp.abs(vertical))
                damping = jnp.exp(jnp.where(vertical < 0.0, -root, 0.0)) * (1.0 / (NX * NY))
                sine, cosine = sin_cos(jnp.where(vertical > 0.0, root, 0.0))
                hcos[k, :, cols] = damping * cosine
                hsin[k, :, cols] = damping * sine
                sine, cosine = sin_cos((ka * kb).astype(f32) * (2 * math.pi / NY))
                tyc[k, :, cols] = cosine
                tys[k, :, cols] = sine

    def make_phase(step):
        @pl.loop(0, ROWS // 8)
        def _(g):
            rows = pl.ds(pl.multiple_of(g * 8, 8), 8)
            for q in range(4):
                cols = slice(q * NX // 4, (q + 1) * NX // 4)
                shift = (omega * layer_thickness) * slow[step, rows, cols]
                sine, cosine = sin_cos(shift)
                phc[step, rows, cols] = cosine
                phs[step, rows, cols] = sine

    def vel_all(sem):
        return remote(vrecv.at[pl.ds(0, FREQ - 1)], vrecv.at[pl.ds(0, FREQ - 1)], vsend.at[0], sem, (f, me))

    def gather_all(step):
        part = slow.at[step, pl.ds(0, (FREQ - 1) * PIECE)]
        return remote(part, part, gsend.at[step], grecv.at[step], (f, me))

    mine8 = pl.ds(pl.multiple_of(f * PIECE, PIECE), PIECE)

    def velocity_start():
        @pl.loop(1, FREQ)
        def _(j):
            p = freq_peer(j)
            rows = pl.ds(pl.multiple_of(p * PIECE, PIECE), PIECE)
            remote(vel_ref.at[rows], vrecv.at[f], vsend.at[0], vrcv.at[0], (p, me)).start()
        pltpu.make_async_copy(vel_ref.at[mine8], vrecv.at[f], vloc.at[0]).start()

    def velocity_share():
        vel_all(vrcv.at[0]).wait_recv()
        pltpu.make_async_copy(vel_ref.at[mine8], vrecv.at[f], vloc.at[0]).wait()
        for step in range(2):
            piece = 1.0 / vrecv[owner_ref[step]] - 1.0 / base_speed
            vsel[step] = piece
            slow[step, mine8] = piece

            @pl.loop(1, FREQ)
            def _(j):
                remote(vsel.at[step], slow.at[step, mine8], gsend.at[step], grecv.at[step], (freq_peer(j), me)).start()

    def image_start(step, ch):
        rows = pl.ds(ch * CHUNK, CHUNK)

        @pl.loop(1, FREQ)
        def _(j):
            p = freq_peer(j)
            cols = pl.ds(pl.multiple_of(p * BAND, BAND), BAND)
            remote(
                terms.at[step, rows, cols], irecv.at[step, f, rows],
                isend.at[step, ch], ircv.at[step, ch], (p, me),
            ).start()

        cols = pl.ds(pl.multiple_of(f * BAND, BAND), BAND)
        pltpu.make_async_copy(terms.at[step, rows, cols], irecv.at[step, f, rows], iloc.at[step, ch]).start()

    def image_all(step, ch):
        part = irecv.at[step, pl.ds(0, FREQ - 1), pl.ds(ch * CHUNK, CHUNK)]
        return remote(part, part, isend.at[step, ch], ircv.at[step, ch], (f, me))

    def image_finish(step, ch):
        rows = pl.ds(ch * CHUNK, CHUNK)
        image_all(step, ch).wait_recv()
        part = irecv.at[step, 0, rows]
        pltpu.make_async_copy(part, part, iloc.at[step, ch]).wait()
        total = irecv[step, 0, rows, :]
        for j in range(1, FREQ):
            total = total + irecv[step, j, rows, :]
        image_ref[step, rows, :] = total

    velocity_start()
    for ch in range(CHUNKS):
        forward_x(wave_ref.at[0, 0], wave_ref.at[0, 1], sendx.at[0], ch)
        a2a_start(sendx.at[0], recvy.at[0], ch, 0)
    make_tables()
    velocity_share()
    gather_all(0).wait_recv()
    gather_all(1).wait_recv()
    make_phase(0)
    make_phase(1)
    for ch in range(CHUNKS):
        a2a_wait_recv(sendx.at[0], recvy.at[0], ch, 0)
    column_pass(recvy.at[0], sendy.at[0], 1)
    for ch in range(CHUNKS):
        a2a_wait_recv(sendy.at[0], recvx.at[0], ch, 1)
        inverse_x(recvx.at[0], 0, terms.at[0], imag, ch)
        forward_x(terms.at[0], imag, sendx.at[1], ch)
        a2a_start(sendx.at[1], recvy.at[1], ch, 2)
        image_start(0, ch)
    for ch in range(CHUNKS):
        a2a_wait_recv(sendx.at[1], recvy.at[1], ch, 2)
    column_pass(recvy.at[1], sendy.at[1], 3)
    for ch in range(CHUNKS):
        image_finish(0, ch)
    for ch in range(CHUNKS):
        a2a_wait_recv(sendy.at[1], recvx.at[1], ch, 3)
        inverse_x(recvx.at[1], 1, terms.at[1], field_ref.at[0, 1], ch)
        image_start(1, ch)
        rows = slice(ch * CHUNK, (ch + 1) * CHUNK)
        field_ref[0, 0, rows, :] = terms[1, rows, :]
    for ch in range(CHUNKS):
        image_finish(1, ch)

    vel_all(vrcv.at[0]).wait_send()
    for step in range(2):
        remote(slow.at[step, pl.ds(0, (FREQ - 1) * PIECE)], slow.at[step, pl.ds(0, (FREQ - 1) * PIECE)], gsend.at[step], grecv.at[step], (f, me)).wait_send()
    for ch in range(CHUNKS):
        for i in range(4):
            src = (sendx if i % 2 == 0 else sendy).at[i // 2]
            a2a_all(src, src, ch, i).wait_send()
        for step in range(2):
            image_all(step, ch).wait_send()


def tables():
    n = np.arange(LANES)
    angle = 2 * np.pi * ((n[:, None] * n[None, :]) % LANES) / LANES
    c, s = np.cos(angle), np.sin(angle)
    right = np.block([[c, -s], [s, c]])
    out = []
    for m in (right, right.T):
        high = m.astype(ml_dtypes.bfloat16)
        out += [high, (m - high.astype(np.float64)).astype(ml_dtypes.bfloat16)]
    tx = 2 * np.pi * ((np.arange(TILES)[:, None] * n[None, :]) % NX) / NX
    return [np.cos(tx).astype(np.float32), np.sin(tx).astype(np.float32)] + out


def shards(wavefield, velocity, freq_index, owner):
    vmem = pl.BlockSpec(memory_space=pltpu.VMEM)
    smem = pl.BlockSpec(memory_space=pltpu.SMEM)
    dma = pltpu.SemaphoreType.DMA
    big = (SPACE, ROWS, 2 * LANES)
    image, field = pl.pallas_call(
        kernel,
        out_shape=(
            jax.ShapeDtypeStruct((2, ROWS, BAND), f32),
            jax.ShapeDtypeStruct((1, 2, ROWS, NX), f32),
        ),
        in_specs=[smem, smem] + [vmem] * 8,
        out_specs=(vmem, vmem),
        scratch_shapes=[
            pltpu.VMEM((TILES, CHUNK, 2 * LANES), f32),
            pltpu.VMEM((2,) + big, f32),
            pltpu.VMEM((2,) + big, f32),
            pltpu.VMEM((2,) + big, f32),
            pltpu.VMEM((2,) + big, f32),
            pltpu.VMEM((YA // 2, 2 * LANES, 2 * LANES), f32),
            pltpu.VMEM((YA // 2, LANES, 2 * LANES), f32),
            pltpu.VMEM((YA // 2, LANES, 2 * LANES), f32),
            pltpu.VMEM((YA // 2, LANES, 2 * LANES), f32),
            pltpu.VMEM((YA // 2, LANES, 2 * LANES), f32),
            pltpu.VMEM((FREQ, PIECE, NX), f32),
            pltpu.VMEM((2, PIECE, NX), f32),
            pltpu.VMEM((2, ROWS, NX), f32),
            pltpu.VMEM((2, ROWS, NX), f32),
            pltpu.VMEM((2, ROWS, NX), f32),
            pltpu.VMEM((2, ROWS, NX), f32),
            pltpu.VMEM((ROWS, NX), f32),
            pltpu.VMEM((2, FREQ, ROWS, BAND), f32),
            dma((4, CHUNKS)), dma((4, CHUNKS)), dma((4, CHUNKS)),
            dma((1,)), dma((1,)), dma((1,)),
            dma((2,)), dma((2,)),
            dma((2, CHUNKS)), dma((2, CHUNKS)), dma((2, CHUNKS)),
        ],
        compiler_params=pltpu.CompilerParams(
            collective_id=0, has_side_effects=True, vmem_limit_bytes=60 * 2**20
        ),
        name="migrate",
    )(freq_index, owner, wavefield, velocity[0], *tables())
    return image, field


def solution(mesh):
    return jax.shard_map(
        shards,
        mesh=mesh,
        in_specs=(P("freq", None, "space", None), P("freq", "space", None), P("freq"), P()),
        out_specs=(P(None, "space", "freq"), P("freq", None, "space", None)),
        check_vma=False,
    )
```

```python
import functools
import math

import jax
import jax.numpy as jnp
import ml_dtypes
import numpy as np
from jax import lax
from jax.experimental import pallas as pl
from jax.experimental.pallas import tpu as pltpu
from jax.sharding import PartitionSpec as P

NX, NY = 4096, 2048
SPACE, FREQ = 32, 8
ROWS = NY // SPACE
LANES = 128
TILES = NX // LANES
YA = NY // LANES
CHUNK = 32
CHUNKS = ROWS // CHUNK
BAND = NX // FREQ
PIECE = ROWS // FREQ

cell_spacing = 25.0
layer_thickness = 10.0
base_speed = 1500.0
lowest_hertz = 5.0
hertz_step = 0.9
MESH = pl.DeviceIdType.MESH
f32 = jnp.float32
bf16 = jnp.bfloat16


def times_root(value, power, length, sign):
    re, im = value
    power = power % length
    quarter = 4 * power
    if quarter % length == 0:
        turn = quarter // length
        if sign < 0:
            turn = (4 - turn) % 4
        return [(re, im), (-im, re), (-re, -im), (im, -re)][turn]
    angle = sign * 2 * math.pi * power / length
    c, s = math.cos(angle), math.sin(angle)
    if (8 * power) % length == 0:
        h = math.sqrt(0.5)
        cs, ss = math.copysign(1, c), math.copysign(1, s)
        p, q = re * h, im * h
        real = (p if cs > 0 else -p) + (-q if ss > 0 else q)
        imag = (p if ss > 0 else -p) + (q if cs > 0 else -q)
        return (real, imag)
    return (re * c - im * s, re * s + im * c)


def add(a, b):
    return (a[0] + b[0], a[1] + b[1])


def sub(a, b):
    return (a[0] - b[0], a[1] - b[1])


def small_dft(values, sign):
    n = len(values)
    if n == 1:
        return values
    if n == 2:
        return [add(values[0], values[1]), sub(values[0], values[1])]
    m = n // 4
    parts = [small_dft(values[r::4], sign) for r in range(4)]
    out = [None] * n
    for k in range(m):
        a = parts[0][k]
        b, c, d = (times_root(parts[r][k], r * k, n, sign) for r in (1, 2, 3))
        s0, s1 = add(a, c), sub(a, c)
        s2, s3 = add(b, d), times_root(sub(b, d), 1, 4, sign)
        out[k], out[k + m] = add(s0, s2), add(s1, s3)
        out[k + 2 * m], out[k + 3 * m] = sub(s0, s2), sub(s1, s3)
    return out


def sin_cos(t):
    n = jnp.floor(t * (2 / math.pi) + 0.5)
    r = (t - n * 1.5703125) - n * 4.83826794896e-4
    z = r * r
    s = r + r * z * (-1.6666654611e-1 + z * (8.3321608736e-3 + z * -1.9515295891e-4))
    c = 1.0 - 0.5 * z + z * z * (4.166664568298827e-2 + z * (-1.388731625493765e-3 + z * 2.443315711809948e-5))
    half = n * 0.5
    odd = half != jnp.floor(half)
    quad = n - 4.0 * jnp.floor(n * 0.25)
    sine = jnp.where(odd, c, s)
    cosine = jnp.where(odd, s, c)
    sine = jnp.where(quad >= 2.0, -sine, sine)
    cosine = jnp.where((quad == 1.0) | (quad == 2.0), -cosine, cosine)
    return sine, cosine


def split(value):
    high = value.astype(bf16)
    return high, (value - high.astype(f32)).astype(bf16)


def mul3(a, b):
    ah, al = a
    bh, bl = b
    dot = functools.partial(jnp.dot, preferred_element_type=f32)
    return dot(ah, bh) + (dot(al, bh) + dot(ah, bl))


def kernel(
    fidx_ref, owner_ref, wave_ref, vel_ref, txc_ref, txs_ref, rh_ref, rl_ref, lh_ref, ll_ref,
    image_ref, field_ref,
    rowbuf, sendx, sendy, recvy, recvx, relay, mid, hcos, hsin, tyc, tys,
    vrecv, vsel, vpart, vturn, slow, phc, phs, terms, imag, irecv, isum, iback, omega_out, omega_in,
    asend, arecv, aloc, rsend, rrecv, zsend, zrecv, rloc,
    vsend, vrcv, vloc, isend, ircv, iloc, tsend, trecv, tloc,
):
    f = lax.axis_index("freq")
    me = lax.axis_index("space")
    x, zl = f // 2, f % 2
    zh, y, c = me // 8, (me // 2) % 4, me % 2
    z = zh * 2 + zl
    here = (x * 4 + y) * 2 + c

    def dev(dx, dy, dzh, dzl, dc):
        return (dx * 2 + dzl, (dzh * 4 + dy) * 2 + dc)

    def plane(j):
        px, py, pc = (x + j // 8) % 4, (y + (j // 2) % 4) % 4, (c + j % 2) % 2
        return dev(px, py, zh, zl, pc), (px * 4 + py) * 2 + pc

    def along_z(j):
        pz = (z + j) % 8
        return dev(x, y, pz // 2, pz % 2, c), pz

    across = dev(zh, y, x, zl, c)
    across_odd = dev(zh, y, x, 1 - zl, c)

    barrier = pltpu.get_barrier_semaphore()

    def greet(device):
        pl.semaphore_signal(barrier, inc=1, device_id=device, device_id_type=MESH)

    @pl.loop(1, 32)
    def _(j):
        greet(plane(j)[0])

    @pl.loop(1, 8)
    def _(j):
        greet(along_z(j)[0])

    @pl.loop(1, 4)
    def _(j):
        greet(dev((x + j) % 4, y, zh, 1 - zl, c))

    greet(across_odd)

    @pl.when(x != zh)
    def _():
        greet(across)

    @pl.when(x == zh)
    def _():
        greet(across_odd)

    pl.semaphore_wait(barrier, 31 + 7 + 3 + 1 + 1)

    def remote(src, dst, send, recv, device):
        return pltpu.make_async_remote_copy(
            src_ref=src, dst_ref=dst, send_sem=send, recv_sem=recv, device_id=device, device_id_type=MESH
        )

    def chunk_rows(ch):
        return pl.ds(ch * CHUNK, CHUNK)

    def a2a_start(src, dst, ch, i):
        rows = chunk_rows(ch)

        @pl.loop(1, 32)
        def _(j):
            device, place = plane(j)
            remote(src.at[place, rows], dst.at[here, rows], asend.at[i, ch], arecv.at[i, ch], device).start()

        pltpu.make_async_copy(src.at[here, rows], dst.at[here, rows], aloc.at[i, ch]).start()

    def a2a_all(dst, ch, i):
        part = dst.at[pl.ds(0, SPACE - 1), chunk_rows(ch)]
        return remote(part, part, asend.at[i, ch], arecv.at[i, ch], across_odd)

    def a2a_wait_recv(dst, ch, i):
        a2a_all(dst, ch, i).wait_recv()
        part = dst.at[here, chunk_rows(ch)]
        pltpu.make_async_copy(part, part, aloc.at[i, ch]).wait()

    def spread_start(src):
        @pl.loop(0, 32)
        def _(j):
            px, py, pc = (x + (j + zh) % 4) % 4, (y + j // 8) % 4, (c + (j // 4) % 2) % 2
            place = (px * 4 + py) * 2 + pc

            @pl.when(place != here)
            def _():
                remote(src.at[place], relay.at[0, j], rsend.at[0], rrecv.at[0, j], dev(px, py, zh, zl, pc)).start()

    def spread_relay(src, dst):
        @pl.loop(0, 32)
        def _(j):
            px, py, pc = (x + 4 - (j + zh) % 4) % 4, (y + 4 - j // 8) % 4, (c + (j // 4) % 2) % 2
            place = (px * 4 + py) * 2 + pc
            slot = (zh * 4 + py) * 2 + pc
            target = dev(x, y, px, 1 - zl, c)

            @pl.when(place == here)
            def _():
                remote(src.at[here], dst.at[slot], zsend.at[0], zrecv.at[0], target).start()

            @pl.when(place != here)
            def _():
                remote(relay.at[0, j], relay.at[0, j], rsend.at[0], rrecv.at[0, j], across_odd).wait_recv()
                remote(relay.at[0, j], dst.at[slot], zsend.at[0], zrecv.at[0], target).start()

    def collect_start(src, ch):
        rows = chunk_rows(ch)

        @pl.loop(0, 32)
        def _(j):
            pzh, py, pc = (zh + j + x) % 4, (y + j // 8) % 4, (c + (j // 4) % 2) % 2
            remote(
                src.at[(pzh * 4 + py) * 2 + pc, rows], relay.at[1, j, rows],
                zsend.at[1 + ch], rrecv.at[1 + ch, j], dev(x, y, pzh, 1 - zl, c),
            ).start()

    def collect_relay(dst, ch, low, high):
        rows = chunk_rows(ch)

        @pl.loop(low, high)
        def _(j):
            px, py, pc = (zh + 64 - j - x) % 4, (y + j // 8) % 4, (c + (j // 4) % 2) % 2
            place = (px * 4 + py) * 2 + pc
            part = relay.at[1, j, rows]
            remote(part, part, zsend.at[1 + ch], rrecv.at[1 + ch, j], across_odd).wait_recv()

            @pl.when(place == here)
            def _():
                pltpu.make_async_copy(part, dst.at[here, rows], rloc.at[ch]).start()

            @pl.when(place != here)
            def _():
                remote(part, dst.at[here, rows], rsend.at[1 + ch], zrecv.at[1 + ch], dev(px, py, zh, zl, pc)).start()

    def collect_all(dst, ch):
        part = dst.at[pl.ds(0, SPACE - 1), chunk_rows(ch)]
        return remote(part, part, rsend.at[1 + ch], zrecv.at[1 + ch], across_odd)

    def collect_wait_recv(dst, ch):
        collect_all(dst, ch).wait_recv()
        part = dst.at[here, chunk_rows(ch)]
        pltpu.make_async_copy(part, part, rloc.at[ch]).wait()

    def forward_x(re_ref, im_ref, dst, ch):
        @pl.loop(0, CHUNK // 8)
        def _(g):
            rows = pl.ds(pl.multiple_of(ch * CHUNK + g * 8, 8), 8)
            local = pl.ds(pl.multiple_of(g * 8, 8), 8)
            vals = [
                (re_ref[rows, a * LANES:(a + 1) * LANES], im_ref[rows, a * LANES:(a + 1) * LANES])
                for a in range(TILES)
            ]
            vals = small_dft(vals, -1)
            for k in range(TILES):
                re, im = vals[k]
                c, s = txc_ref[k:k + 1, :], txs_ref[k:k + 1, :]
                rowbuf[k, local, 0:LANES] = re * c + im * s
                rowbuf[k, local, LANES:] = im * c - re * s

        @pl.loop(0, TILES // 8)
        def _(g):
            some = pl.ds(g * 8, 8)
            block = rowbuf[some].reshape(8 * CHUNK, 2 * LANES)
            out = mul3(split(block), (rh_ref[...], rl_ref[...]))
            dst[some, pl.ds(ch * CHUNK, CHUNK), :] = out.reshape(8, CHUNK, 2 * LANES)

    def inverse_x(src, step, re_ref, im_ref, ch):
        @pl.loop(0, TILES // 8)
        def _(g):
            some = pl.ds(g * 8, 8)
            block = src[some, pl.ds(ch * CHUNK, CHUNK), :].reshape(8 * CHUNK, 2 * LANES)
            out = mul3(split(block), (lh_ref[...], ll_ref[...]))
            rowbuf[some] = out.reshape(8, CHUNK, 2 * LANES)

        @pl.loop(0, CHUNK // 8)
        def _(g):
            rows = pl.ds(pl.multiple_of(ch * CHUNK + g * 8, 8), 8)
            local = pl.ds(pl.multiple_of(g * 8, 8), 8)
            vals = []
            for k in range(TILES):
                re, im = rowbuf[k, local, 0:LANES], rowbuf[k, local, LANES:]
                c, s = txc_ref[k:k + 1, :], txs_ref[k:k + 1, :]
                vals.append((re * c - im * s, im * c + re * s))
            vals = small_dft(vals, 1)
            for a in range(TILES):
                re, im = vals[a]
                cols = slice(a * LANES, (a + 1) * LANES)
                c, s = phc[step, rows, cols], phs[step, rows, cols]
                re_ref[rows, cols] = re * c - im * s
                im_ref[rows, cols] = re * s + im * c

    def column_pass(src, dst, send):
        @pl.loop(0, LANES // 8)
        def _(t):
            half, sub_rows = t // 8, pl.ds(pl.multiple_of(t % 8 * 8, 8), 8)
            vals = [
                (src[2 * a + half, sub_rows, 0:LANES], src[2 * a + half, sub_rows, LANES:]) for a in range(YA)
            ]
            vals = small_dft(vals, -1)
            re_rows = pl.ds(pl.multiple_of(t * 8, 8), 8)
            im_rows = pl.ds(pl.multiple_of(LANES + t * 8, 8), 8)
            for k in range(YA):
                re, im = vals[k]
                cols = slice(k % 2 * LANES, k % 2 * LANES + LANES)
                c, s = tyc[k // 2, re_rows, cols], tys[k // 2, re_rows, cols]
                mid[k // 2, re_rows, cols] = re * c + im * s
                mid[k // 2, im_rows, cols] = im * c - re * s

        @pl.loop(0, YA // 2)
        def _(k):
            left = (lh_ref[...], ll_ref[...])
            spec = mul3(left, split(mid[k]))
            re, im = spec[:LANES], spec[LANES:]
            c, s = hcos[k], hsin[k]
            spec = jnp.concatenate([re * c - im * s, re * s + im * c], axis=0)
            mid[k] = mul3((rh_ref[...], rl_ref[...]), split(spec))

        for ch in range(CHUNKS):
            @pl.loop(0, CHUNK // 4)
            def _(q):
                half, tile = q % 2, ch * (CHUNK // 8) + q // 2
                t = half * 8 + tile
                re_rows = pl.ds(pl.multiple_of(t * 8, 8), 8)
                im_rows = pl.ds(pl.multiple_of(LANES + t * 8, 8), 8)
                vals = []
                for k in range(YA):
                    cols = slice(k % 2 * LANES, k % 2 * LANES + LANES)
                    re, im = mid[k // 2, re_rows, cols], mid[k // 2, im_rows, cols]
                    c, s = tyc[k // 2, re_rows, cols], tys[k // 2, re_rows, cols]
                    vals.append((re * c - im * s, im * c + re * s))
                vals = small_dft(vals, 1)
                out_rows = pl.ds(pl.multiple_of(tile * 8, 8), 8)
                for a in range(YA):
                    dst[2 * a + half, out_rows, 0:LANES] = vals[a][0]
                    dst[2 * a + half, out_rows, LANES:] = vals[a][1]
            send(ch)

    def make_tables(omega):
        kb = lax.broadcasted_iota(jnp.int32, (LANES, LANES), 0)
        lane = lax.broadcasted_iota(jnp.int32, (LANES, LANES), 1)
        jx = here + TILES * lane
        kx = jnp.where(jx < NX // 2, jx, jx - NX).astype(f32) * (2 * math.pi / (NX * cell_spacing))

        @pl.loop(0, YA // 2)
        def _(k):
            for part in range(2):
                ka = 2 * k + part
                cols = slice(part * LANES, (part + 1) * LANES)
                jy = ka + YA * kb
                ky = jnp.where(jy < NY // 2, jy, jy - NY).astype(f32) * (2 * math.pi / (NY * cell_spacing))
                vertical = (omega / base_speed) ** 2 - (ky * ky + kx * kx)
                root = layer_thickness * jnp.sqrt(jnp.abs(vertical))
                damping = jnp.exp(jnp.where(vertical < 0.0, -root, 0.0)) * (1.0 / (NX * NY))
                sine, cosine = sin_cos(jnp.where(vertical > 0.0, root, 0.0))
                hcos[k, :, cols] = damping * cosine
                hsin[k, :, cols] = damping * sine
                sine, cosine = sin_cos((ka * kb).astype(f32) * (2 * math.pi / NY))
                tyc[k, :, cols] = cosine
                tys[k, :, cols] = sine

    def make_phase(step, omega):
        @pl.loop(0, ROWS // 8)
        def _(g):
            rows = pl.ds(pl.multiple_of(g * 8, 8), 8)
            for q in range(4):
                cols = slice(q * NX // 4, (q + 1) * NX // 4)
                shift = (omega * layer_thickness) * slow[step, rows, cols]
                sine, cosine = sin_cos(shift)
                phc[step, rows, cols] = cosine
                phs[step, rows, cols] = sine

    quarter = pl.ds(pl.multiple_of(x * 2 * PIECE, 2 * PIECE), 2 * PIECE)

    def velocity_start():
        @pl.loop(1, 4)
        def _(j):
            px = (x + j) % 4
            rows = pl.ds(pl.multiple_of(px * 2 * PIECE, 2 * PIECE), 2 * PIECE)
            remote(vel_ref.at[rows], vrecv.at[x], vsend.at[0], vrcv.at[0], dev(px, y, zh, zl, c)).start()

        pltpu.make_async_copy(vel_ref.at[quarter], vrecv.at[x], vloc.at[0]).start()

    def velocity_all():
        part = vrecv.at[pl.ds(0, 3)]
        return remote(part, part, vsend.at[0], vrcv.at[0], across_odd)

    partner = dev(x, y, zh, 1 - zl, c)
    own_half = pl.ds(pl.multiple_of(zl * PIECE, PIECE), PIECE)
    other_half = pl.ds(pl.multiple_of((1 - zl) * PIECE, PIECE), PIECE)
    pair0 = remote(vsel.at[0, other_half], vpart.at[0, pl.ds(0, PIECE)], vsend.at[1], vrcv.at[1], partner)
    pair1 = remote(vsel.at[1], vpart.at[1], vsend.at[2], vrcv.at[2], partner)
    turn = remote(vsel.at[2, pl.ds(0, PIECE)], vturn, vsend.at[3], vrcv.at[3], across)
    turn_here = pltpu.make_async_copy(vsel.at[2, pl.ds(0, PIECE)], vturn, vloc.at[1])

    def velocity_select():
        velocity_all().wait_recv()
        pltpu.make_async_copy(vel_ref.at[quarter], vrecv.at[x], vloc.at[0]).wait()
        for step in range(2):
            chosen = owner_ref[step]
            piece = 1.0 / vrecv[chosen // 2] - 1.0 / base_speed
            vsel[step] = jnp.where(chosen % 2 == zl, piece, 0.0)
        pair0.start()
        pair0.wait_recv()
        vsel[2, 0:PIECE] = vsel[0, own_half] + vpart[0, 0:PIECE]

        @pl.when(x != zh)
        def _():
            turn.start()
            turn.wait_recv()

        @pl.when(x == zh)
        def _():
            turn_here.start()
            turn_here.wait()

    eighth = pl.ds(pl.multiple_of(z * PIECE, PIECE), PIECE)

    def velocity_along_z():
        @pl.loop(1, 8)
        def _(j):
            remote(vturn, slow.at[0, eighth], vsend.at[4], vrcv.at[4], along_z(j)[0]).start()

        slow[0, eighth] = vturn[...]
        pair1.start()

    def along_z_all():
        part = slow.at[0, pl.ds(0, 7 * PIECE)]
        return remote(part, part, vsend.at[4], vrcv.at[4], across_odd)

    def velocity_along_x():
        pair1.wait_recv()
        piece = vsel[1] + vpart[1]
        vsel[3] = piece
        slow[1, quarter] = piece

        @pl.loop(1, 4)
        def _(j):
            remote(vsel.at[3], slow.at[1, quarter], vsend.at[5], vrcv.at[5], dev((x + j) % 4, y, zh, zl, c)).start()

    def along_x_all():
        part = slow.at[1, pl.ds(0, 6 * PIECE)]
        return remote(part, part, vsend.at[5], vrcv.at[5], across_odd)

    def image_start(step, ch):
        rows = chunk_rows(ch)
        mine = z if step == 0 else f

        @pl.loop(1, 8)
        def _(j):
            if step == 0:
                device, p = along_z(j)
            else:
                p = (f + j) % 8
                device = (p, me)
            cols = pl.ds(pl.multiple_of(p * BAND, BAND), BAND)
            remote(
                terms.at[step, rows, cols], irecv.at[step, mine, rows],
                isend.at[step, ch], ircv.at[step, ch], device,
            ).start()

        cols = pl.ds(pl.multiple_of(mine * BAND, BAND), BAND)
        pltpu.make_async_copy(terms.at[step, rows, cols], irecv.at[step, mine, rows], iloc.at[step, ch]).start()

    def image_all(step, ch):
        part = irecv.at[step, pl.ds(0, FREQ - 1), chunk_rows(ch)]
        return remote(part, part, isend.at[step, ch], ircv.at[step, ch], across_odd)

    def image_sum(step, ch):
        rows = chunk_rows(ch)
        image_all(step, ch).wait_recv()
        part = irecv.at[step, 0, rows]
        pltpu.make_async_copy(part, part, iloc.at[step, ch]).wait()
        total = irecv[step, 0, rows, :]
        for j in range(1, FREQ):
            total = total + irecv[step, j, rows, :]
        return rows, total

    back = remote(isum, iback, tsend.at[0], trecv.at[0], across)
    back_here = pltpu.make_async_copy(isum, iback, tloc.at[0])

    omega = 2 * math.pi * (lowest_hertz + hertz_step * fidx_ref[0].astype(f32))
    omega_out[...] = jnp.full((8, LANES), omega, f32)
    omega_turn = remote(omega_out, omega_in, tsend.at[1], trecv.at[1], across_odd)
    omega_turn.start()
    for ch in range(CHUNKS):
        forward_x(wave_ref.at[0, 0], wave_ref.at[0, 1], sendx.at[0], ch)
    spread_start(sendx.at[0])
    velocity_start()
    spread_relay(sendx.at[0], recvy.at[0])
    omega_turn.wait_recv()
    omega_col = omega_in[0:1, :]
    make_tables(omega_col)
    velocity_select()
    recvy_all = remote(recvy.at[0], recvy.at[0], zsend.at[0], zrecv.at[0], across_odd)
    recvy_all.wait_recv()
    velocity_along_z()
    column_pass(recvy.at[0], sendy.at[0], lambda ch: a2a_start(sendy.at[0], recvx.at[0], ch, 0))
    along_z_all().wait_recv()
    make_phase(0, omega_in[0:1, 0:1])
    for ch in range(CHUNKS):
        a2a_wait_recv(recvx.at[0], ch, 0)
        inverse_x(recvx.at[0], 0, terms.at[0], imag, ch)
        forward_x(terms.at[0], imag, sendx.at[1], ch)
        a2a_start(sendx.at[1], recvy.at[1], ch, 1)
        image_start(0, ch)
    for ch in range(CHUNKS):
        a2a_wait_recv(recvy.at[1], ch, 1)
    column_pass(recvy.at[1], sendy.at[1], lambda ch: collect_start(sendy.at[1], ch))
    velocity_along_x()
    for ch in range(CHUNKS):
        rows, total = image_sum(0, ch)
        isum[rows, :] = total

    @pl.when(x != zh)
    def _():
        back.start()

    @pl.when(x == zh)
    def _():
        back_here.start()

    def finish(ch):
        collect_wait_recv(recvx.at[1], ch)
        inverse_x(recvx.at[1], 1, terms.at[1], field_ref.at[0, 1], ch)
        image_start(1, ch)
        rows = chunk_rows(ch)
        field_ref[0, 0, rows, :] = terms[1, rows, :]

    collect_relay(recvx.at[1], 0, 0, 32)
    along_x_all().wait_recv()
    make_phase(1, omega)
    for ch in range(1, CHUNKS):
        collect_relay(recvx.at[1], ch, 0, 16)
        finish(ch - 1)
        collect_relay(recvx.at[1], ch, 16, 32)
    finish(CHUNKS - 1)

    @pl.when(x != zh)
    def _():
        back.wait()
        turn.wait_send()

    @pl.when(x == zh)
    def _():
        back_here.wait()

    image_ref[0] = iback[...]
    for ch in range(CHUNKS):
        rows, total = image_sum(1, ch)
        image_ref[1, rows, :] = total

    omega_turn.wait_send()
    remote(relay.at[0, pl.ds(0, 31)], relay.at[0, pl.ds(0, 31)], rsend.at[0], rrecv.at[0, 0], across_odd).wait_send()
    recvy_all.wait_send()
    velocity_all().wait_send()
    pair0.wait_send()
    pair1.wait_send()
    along_z_all().wait_send()
    along_x_all().wait_send()
    for ch in range(CHUNKS):
        part = relay.at[1, :, chunk_rows(ch)]
        remote(part, part, zsend.at[1 + ch], rrecv.at[1 + ch, 0], across_odd).wait_send()
        collect_all(recvx.at[1], ch).wait_send()
        for i in range(2):
            a2a_all(recvx.at[0], ch, i).wait_send()
            image_all(i, ch).wait_send()


def tables():
    n = np.arange(LANES)
    angle = 2 * np.pi * ((n[:, None] * n[None, :]) % LANES) / LANES
    c, s = np.cos(angle), np.sin(angle)
    right = np.block([[c, -s], [s, c]])
    out = []
    for m in (right, right.T):
        high = m.astype(ml_dtypes.bfloat16)
        out += [high, (m - high.astype(np.float64)).astype(ml_dtypes.bfloat16)]
    tx = 2 * np.pi * ((np.arange(TILES)[:, None] * n[None, :]) % NX) / NX
    return [np.cos(tx).astype(np.float32), np.sin(tx).astype(np.float32)] + out


def shards(wavefield, velocity, freq_index, owner):
    vmem = pl.BlockSpec(memory_space=pltpu.VMEM)
    smem = pl.BlockSpec(memory_space=pltpu.SMEM)
    dma = pltpu.SemaphoreType.DMA
    big = (SPACE, ROWS, 2 * LANES)
    image, field = pl.pallas_call(
        kernel,
        out_shape=(
            jax.ShapeDtypeStruct((2, ROWS, BAND), f32),
            jax.ShapeDtypeStruct((1, 2, ROWS, NX), f32),
        ),
        in_specs=[smem, smem] + [vmem] * 8,
        out_specs=(vmem, vmem),
        scratch_shapes=[
            pltpu.VMEM((TILES, CHUNK, 2 * LANES), f32),
            pltpu.VMEM((2,) + big, f32),
            pltpu.VMEM((2,) + big, f32),
            pltpu.VMEM((2,) + big, f32),
            pltpu.VMEM((2,) + big, f32),
            pltpu.VMEM((2,) + big, f32),
            pltpu.VMEM((YA // 2, 2 * LANES, 2 * LANES), f32),
            pltpu.VMEM((YA // 2, LANES, 2 * LANES), f32),
            pltpu.VMEM((YA // 2, LANES, 2 * LANES), f32),
            pltpu.VMEM((YA // 2, LANES, 2 * LANES), f32),
            pltpu.VMEM((YA // 2, LANES, 2 * LANES), f32),
            pltpu.VMEM((4, 2 * PIECE, NX), f32),
            pltpu.VMEM((4, 2 * PIECE, NX), f32),
            pltpu.VMEM((2, 2 * PIECE, NX), f32),
            pltpu.VMEM((PIECE, NX), f32),
            pltpu.VMEM((2, ROWS, NX), f32),
            pltpu.VMEM((2, ROWS, NX), f32),
            pltpu.VMEM((2, ROWS, NX), f32),
            pltpu.VMEM((2, ROWS, NX), f32),
            pltpu.VMEM((ROWS, NX), f32),
            pltpu.VMEM((2, FREQ, ROWS, BAND), f32),
            pltpu.VMEM((ROWS, BAND), f32),
            pltpu.VMEM((ROWS, BAND), f32),
            pltpu.VMEM((8, LANES), f32),
            pltpu.VMEM((8, LANES), f32),
            dma((2, CHUNKS)), dma((2, CHUNKS)), dma((2, CHUNKS)),
            dma((1 + CHUNKS,)), dma((1 + CHUNKS, 32)), dma((1 + CHUNKS,)), dma((1 + CHUNKS,)), dma((CHUNKS,)),
            dma((6,)), dma((6,)), dma((2,)),
            dma((2, CHUNKS)), dma((2, CHUNKS)), dma((2, CHUNKS)),
            dma((2,)), dma((2,)), dma((1,)),
        ],
        compiler_params=pltpu.CompilerParams(
            collective_id=0, has_side_effects=True, vmem_limit_bytes=60 * 2**20
        ),
        name="migrate",
    )(freq_index, owner, wavefield, velocity[0], *tables())
    return image, field


def solution(mesh):
    return jax.shard_map(
        shards,
        mesh=mesh,
        in_specs=(P("freq", None, "space", None), P("freq", "space", None), P("freq"), P()),
        out_specs=(P(None, "space", "freq"), P("freq", None, "space", None)),
        check_vma=False,
    )
```

```python
import functools
import math

import jax
import jax.numpy as jnp
import ml_dtypes
import numpy as np
from jax import lax
from jax.experimental import pallas as pl
from jax.experimental.pallas import tpu as pltpu
from jax.sharding import PartitionSpec as P

NX, NY = 4096, 2048
SPACE, FREQ = 32, 8
ROWS = NY // SPACE
LANES = 128
TILES = NX // LANES
YA = NY // LANES
CHUNK = 32
CHUNKS = ROWS // CHUNK
BAND = NX // FREQ
PIECE = ROWS // FREQ
AHEAD, BEHIND, WINDOW = 16, 16, 16

cell_spacing = 25.0
layer_thickness = 10.0
base_speed = 1500.0
lowest_hertz = 5.0
hertz_step = 0.9
MESH = pl.DeviceIdType.MESH
f32 = jnp.float32
bf16 = jnp.bfloat16


def times_root(value, power, length, sign):
    re, im = value
    power = power % length
    quarter = 4 * power
    if quarter % length == 0:
        turn = quarter // length
        if sign < 0:
            turn = (4 - turn) % 4
        return [(re, im), (-im, re), (-re, -im), (im, -re)][turn]
    angle = sign * 2 * math.pi * power / length
    c, s = math.cos(angle), math.sin(angle)
    if (8 * power) % length == 0:
        h = math.sqrt(0.5)
        cs, ss = math.copysign(1, c), math.copysign(1, s)
        p, q = re * h, im * h
        real = (p if cs > 0 else -p) + (-q if ss > 0 else q)
        imag = (p if ss > 0 else -p) + (q if cs > 0 else -q)
        return (real, imag)
    return (re * c - im * s, re * s + im * c)


def add(a, b):
    return (a[0] + b[0], a[1] + b[1])


def sub(a, b):
    return (a[0] - b[0], a[1] - b[1])


def small_dft(values, sign):
    n = len(values)
    if n == 1:
        return values
    if n == 2:
        return [add(values[0], values[1]), sub(values[0], values[1])]
    m = n // 4
    parts = [small_dft(values[r::4], sign) for r in range(4)]
    out = [None] * n
    for k in range(m):
        a = parts[0][k]
        b, c, d = (times_root(parts[r][k], r * k, n, sign) for r in (1, 2, 3))
        s0, s1 = add(a, c), sub(a, c)
        s2, s3 = add(b, d), times_root(sub(b, d), 1, 4, sign)
        out[k], out[k + m] = add(s0, s2), add(s1, s3)
        out[k + 2 * m], out[k + 3 * m] = sub(s0, s2), sub(s1, s3)
    return out


def sin_cos(t):
    n = jnp.floor(t * (2 / math.pi) + 0.5)
    r = (t - n * 1.5703125) - n * 4.83826794896e-4
    z = r * r
    s = r + r * z * (-1.6666654611e-1 + z * (8.3321608736e-3 + z * -1.9515295891e-4))
    c = 1.0 - 0.5 * z + z * z * (4.166664568298827e-2 + z * (-1.388731625493765e-3 + z * 2.443315711809948e-5))
    half = n * 0.5
    odd = half != jnp.floor(half)
    quad = n - 4.0 * jnp.floor(n * 0.25)
    sine = jnp.where(odd, c, s)
    cosine = jnp.where(odd, s, c)
    sine = jnp.where(quad >= 2.0, -sine, sine)
    cosine = jnp.where((quad == 1.0) | (quad == 2.0), -cosine, cosine)
    return sine, cosine


def split(value):
    high = value.astype(bf16)
    return high, (value - high.astype(f32)).astype(bf16)


def mul3(a, b):
    ah, al = a
    bh, bl = b
    dot = functools.partial(jnp.dot, preferred_element_type=f32)
    return dot(ah, bh) + (dot(al, bh) + dot(ah, bl))


def left_mul3(left_ref, b):
    bh, bl = b
    n = bh.shape[0]
    dot = functools.partial(jnp.dot, preferred_element_type=f32)
    both = dot(left_ref[...], bh)
    return both[:n] + (both[n:] + dot(left_ref[:n, :], bl))


def kernel(
    fidx_ref, owner_ref, wave_ref, vel_ref, txc_ref, txs_ref, rh_ref, rl_ref, lh_ref, ll_ref, rs_ref, ls_ref,
    image_ref, field_ref,
    rowbuf, sendx, sendy, recvy, recvx, relay, mid, hcos, hsin, tyc, tys,
    vrecv, vsel, vpart, vturn, slow, phc, phs, terms, imag, irecv, isum, iback, omega_out, omega_in,
    asend, arecv, aloc, rsend, rrecv, zsend, zrecv, rloc,
    vsend, vrcv, vloc, isend, ircv, iloc, tsend, trecv, tloc, gate, csend, psend,
):
    f = lax.axis_index("freq")
    me = lax.axis_index("space")
    x, zl = f // 2, f % 2
    zh, y, c = me // 8, (me // 2) % 4, me % 2
    z = zh * 2 + zl
    here = (x * 4 + y) * 2 + c

    def dev(dx, dy, dzh, dzl, dc):
        return (dx * 2 + dzl, (dzh * 4 + dy) * 2 + dc)

    def plane(j):
        px, py, pc = (x + j % 4) % 4, (y + j // 4 + j) % 4, (c + j // 16) % 2
        return dev(px, py, zh, zl, pc), (px * 4 + py) * 2 + pc

    def along_z(j):
        pz = (z + j) % 8
        return dev(x, y, pz // 2, pz % 2, c), pz

    other_core = dev(x, y, zh, zl, 1 - c)
    across = dev(zh, y, x, zl, c)
    across_odd = dev(zh, y, x, 1 - zl, c)

    barrier = pltpu.get_barrier_semaphore()

    def greet(device):
        pl.semaphore_signal(barrier, inc=1, device_id=device, device_id_type=MESH)

    @pl.loop(1, 32)
    def _(j):
        greet(plane(j)[0])

    @pl.loop(1, 8)
    def _(j):
        greet(along_z(j)[0])

    @pl.loop(1, 4)
    def _(j):
        greet(dev((x + j) % 4, y, zh, 1 - zl, c))

    greet(across_odd)

    @pl.when(x != zh)
    def _():
        greet(across)

    @pl.when(x == zh)
    def _():
        greet(across_odd)

    def remote(src, dst, send, recv, device):
        return pltpu.make_async_remote_copy(
            src_ref=src, dst_ref=dst, send_sem=send, recv_sem=recv, device_id=device, device_id_type=MESH
        )

    def chunk_rows(ch):
        return pl.ds(ch * CHUNK, CHUNK)

    def a2a_start(src, dst, ch, i):
        rows = chunk_rows(ch)

        @pl.loop(1, 32)
        def _(j):
            device, place = plane(j)
            remote(src.at[place, rows], dst.at[here, rows], asend.at[i, ch], arecv.at[i, ch], device).start()

        pltpu.make_async_copy(src.at[here, rows], dst.at[here, rows], aloc.at[i, ch]).start()

    def a2a_start_core(src, dst, ch, i, core):
        rows = chunk_rows(ch)

        @pl.loop(0, 16)
        def _(k):
            px, py = (x + k % 4) % 4, (y + k // 4 + k) % 4
            place = (px * 4 + py) * 2 + core

            @pl.when(place != here)
            def _():
                remote(
                    src.at[place, rows], dst.at[here, rows], csend.at[core, ch], arecv.at[i, ch],
                    dev(px, py, zh, zl, core),
                ).start()

            @pl.when(place == here)
            def _():
                pltpu.make_async_copy(src.at[here, rows], dst.at[here, rows], aloc.at[i, ch]).start()

    def a2a_core_sent(dst, ch, i, core):
        @pl.when(c == core)
        def _():
            part = dst.at[pl.ds(0, 15), chunk_rows(ch)]
            remote(part, part, csend.at[core, ch], arecv.at[i, ch], across_odd).wait_send()

        @pl.when(c != core)
        def _():
            part = dst.at[pl.ds(0, 16), chunk_rows(ch)]
            remote(part, part, csend.at[core, ch], arecv.at[i, ch], across_odd).wait_send()

    def a2a_all(dst, ch, i):
        part = dst.at[pl.ds(0, SPACE - 1), chunk_rows(ch)]
        return remote(part, part, asend.at[i, ch], arecv.at[i, ch], across_odd)

    def a2a_wait_recv(dst, ch, i):
        a2a_all(dst, ch, i).wait_recv()
        part = dst.at[here, chunk_rows(ch)]
        pltpu.make_async_copy(part, part, aloc.at[i, ch]).wait()

    def spread_send(src, q, sent=False):
        k, pc = q % 16, q // 16
        px, py = (x + k + zh) % 4, (y + k // 4 + k) % 4
        place, slot = (px * 4 + py) * 2 + pc, k * 2 + c

        @pl.when(place != here)
        def _():
            copy = remote(
                src.at[place], relay.at[0, slot], psend.at[q], rrecv.at[0, slot], dev(px, py, zh, zl, pc)
            )
            if sent:
                copy.wait_send()
            else:
                copy.start()

    def spread_relay(src, dst, r):
        k, pc = r // 2, r % 2
        px, py = (x + 64 - k - zh) % 4, (y + 64 - k // 4 - k) % 4
        place, slot = (px * 4 + py) * 2 + pc, (zh * 4 + py) * 2 + pc
        target = dev(x, y, px, 1 - zl, c)

        @pl.when(place == here)
        def _():
            remote(src.at[here], dst.at[slot], zsend.at[0], zrecv.at[0], target).start()

        @pl.when(place != here)
        def _():
            remote(relay.at[0, r], relay.at[0, r], rsend.at[0], rrecv.at[0, r], across_odd).wait_recv()
            remote(relay.at[0, r], dst.at[slot], zsend.at[0], zrecv.at[0], target).start()

    def spread(src, dst):
        ahead = AHEAD + (32 - AHEAD) * c

        @pl.loop(0, ahead)
        def _(q):
            @pl.when(q >= WINDOW)
            def _():
                spread_send(src, q - WINDOW, True)

            spread_send(src, q)

        @pl.when(c == 1)
        def _():
            @pl.loop(32 - WINDOW, 32)
            def _(q):
                spread_send(src, q, True)

            velocity_start()
            pl.semaphore_wait(gate.at[0], 1)

        @pl.loop(0, 32)
        def _(r):
            spread_relay(src, dst, r)

            @pl.when((c == 0) & (r == 12))
            def _():
                velocity_start()

            @pl.when(ahead + r < 32)
            def _():
                spread_send(src, ahead + r - WINDOW, True)
                spread_send(src, ahead + r)

        @pl.when(c == 0)
        def _():
            @pl.loop(32 - WINDOW, 32)
            def _(q):
                spread_send(src, q, True)

            pl.semaphore_signal(gate.at[0], inc=1, device_id=other_core, device_id_type=MESH)

    def collect_send(src, i):
        ch, j = i // 32, i % 32
        rows = pl.ds(pl.multiple_of(ch * CHUNK, CHUNK), CHUNK)
        pzh, py, pc = (zh + j + x) % 4, (y + j // 8) % 4, (c + (j // 4) % 2) % 2
        remote(
            src.at[(pzh * 4 + py) * 2 + pc, rows], relay.at[1, j, rows],
            zsend.at[1 + ch], rrecv.at[1 + ch, j], dev(x, y, pzh, 1 - zl, c),
        ).start()

    def collect_relay(dst, i):
        ch, j = i // 32, i % 32
        rows = pl.ds(pl.multiple_of(ch * CHUNK, CHUNK), CHUNK)
        px, py, pc = (zh + 64 - j - x) % 4, (y + j // 8) % 4, (c + (j // 4) % 2) % 2
        place = (px * 4 + py) * 2 + pc
        part = relay.at[1, j, rows]
        remote(part, part, zsend.at[1 + ch], rrecv.at[1 + ch, j], across_odd).wait_recv()

        @pl.when(place == here)
        def _():
            pltpu.make_async_copy(part, dst.at[here, rows], rloc.at[ch]).start()

        @pl.when(place != here)
        def _():
            remote(part, dst.at[here, rows], rsend.at[1 + ch], zrecv.at[1 + ch], dev(px, py, zh, zl, pc)).start()

    def collect(src, dst, low, high):
        @pl.loop(low, high)
        def _(i):
            collect_relay(dst, i)

            @pl.when(BEHIND + i < 32 * CHUNKS)
            def _():
                collect_send(src, BEHIND + i)

    def collect_all(dst, ch):
        part = dst.at[pl.ds(0, SPACE - 1), chunk_rows(ch)]
        return remote(part, part, rsend.at[1 + ch], zrecv.at[1 + ch], across_odd)

    def collect_wait_recv(dst, ch):
        collect_all(dst, ch).wait_recv()
        part = dst.at[here, chunk_rows(ch)]
        pltpu.make_async_copy(part, part, rloc.at[ch]).wait()

    def forward_x(re_ref, im_ref, dst, ch):
        @pl.loop(0, CHUNK // 8)
        def _(g):
            rows = pl.ds(pl.multiple_of(ch * CHUNK + g * 8, 8), 8)
            local = pl.ds(pl.multiple_of(g * 8, 8), 8)
            vals = [
                (re_ref[rows, a * LANES:(a + 1) * LANES], im_ref[rows, a * LANES:(a + 1) * LANES])
                for a in range(TILES)
            ]
            vals = small_dft(vals, -1)
            for k in range(TILES):
                re, im = vals[k]
                c, s = txc_ref[k:k + 1, :], txs_ref[k:k + 1, :]
                rowbuf[k, local, 0:LANES] = re * c + im * s
                rowbuf[k, local, LANES:] = im * c - re * s

        @pl.loop(0, TILES // 8)
        def _(g):
            some = pl.ds(g * 8, 8)
            block = rowbuf[some].reshape(8 * CHUNK, 2 * LANES)
            out = mul3(split(block), (rh_ref[...], rl_ref[...]))
            dst[some, pl.ds(ch * CHUNK, CHUNK), :] = out.reshape(8, CHUNK, 2 * LANES)

    def inverse_x(src, step, re_ref, im_ref, ch):
        @pl.loop(0, TILES // 8)
        def _(g):
            some = pl.ds(g * 8, 8)
            block = src[some, pl.ds(ch * CHUNK, CHUNK), :].reshape(8 * CHUNK, 2 * LANES)
            out = mul3(split(block), (lh_ref[...], ll_ref[...]))
            rowbuf[some] = out.reshape(8, CHUNK, 2 * LANES)

        @pl.loop(0, CHUNK // 8)
        def _(g):
            rows = pl.ds(pl.multiple_of(ch * CHUNK + g * 8, 8), 8)
            local = pl.ds(pl.multiple_of(g * 8, 8), 8)
            vals = []
            for k in range(TILES):
                re, im = rowbuf[k, local, 0:LANES], rowbuf[k, local, LANES:]
                c, s = txc_ref[k:k + 1, :], txs_ref[k:k + 1, :]
                vals.append((re * c - im * s, im * c + re * s))
            vals = small_dft(vals, 1)
            for a in range(TILES):
                re, im = vals[a]
                cols = slice(a * LANES, (a + 1) * LANES)
                c, s = phc[step, rows, cols], phs[step, rows, cols]
                re_ref[rows, cols] = re * c - im * s
                im_ref[rows, cols] = re * s + im * c

    def column_pass(src, dst, send):
        @pl.loop(0, LANES // 8)
        def _(t):
            half, sub_rows = t // 8, pl.ds(pl.multiple_of(t % 8 * 8, 8), 8)
            vals = [
                (src[2 * a + half, sub_rows, 0:LANES], src[2 * a + half, sub_rows, LANES:]) for a in range(YA)
            ]
            vals = small_dft(vals, -1)
            re_rows = pl.ds(pl.multiple_of(t * 8, 8), 8)
            im_rows = pl.ds(pl.multiple_of(LANES + t * 8, 8), 8)
            for k in range(YA):
                re, im = vals[k]
                cols = slice(k % 2 * LANES, k % 2 * LANES + LANES)
                c, s = tyc[k // 2, re_rows, cols], tys[k // 2, re_rows, cols]
                mid[k // 2, re_rows, cols] = re * c + im * s
                mid[k // 2, im_rows, cols] = im * c - re * s

        @pl.loop(0, YA // 2)
        def _(k):
            spec = left_mul3(ls_ref, split(mid[k]))
            re, im = spec[:LANES], spec[LANES:]
            c, s = hcos[k], hsin[k]
            spec = jnp.concatenate([re * c - im * s, re * s + im * c], axis=0)
            mid[k] = left_mul3(rs_ref, split(spec))

        for ch in range(CHUNKS):
            @pl.loop(0, CHUNK // 4)
            def _(q):
                half, tile = q % 2, ch * (CHUNK // 8) + q // 2
                t = half * 8 + tile
                re_rows = pl.ds(pl.multiple_of(t * 8, 8), 8)
                im_rows = pl.ds(pl.multiple_of(LANES + t * 8, 8), 8)
                vals = []
                for k in range(YA):
                    cols = slice(k % 2 * LANES, k % 2 * LANES + LANES)
                    re, im = mid[k // 2, re_rows, cols], mid[k // 2, im_rows, cols]
                    c, s = tyc[k // 2, re_rows, cols], tys[k // 2, re_rows, cols]
                    vals.append((re * c - im * s, im * c + re * s))
                vals = small_dft(vals, 1)
                out_rows = pl.ds(pl.multiple_of(tile * 8, 8), 8)
                for a in range(YA):
                    dst[2 * a + half, out_rows, 0:LANES] = vals[a][0]
                    dst[2 * a + half, out_rows, LANES:] = vals[a][1]
            send(ch)

    def make_twiddles():
        kb = lax.broadcasted_iota(jnp.int32, (LANES, LANES), 0)

        @pl.loop(0, YA // 2)
        def _(k):
            for part in range(2):
                cols = slice(part * LANES, (part + 1) * LANES)
                sine, cosine = sin_cos(((2 * k + part) * kb).astype(f32) * (2 * math.pi / NY))
                tyc[k, :, cols] = cosine
                tys[k, :, cols] = sine

    def make_tables(omega):
        kb = lax.broadcasted_iota(jnp.int32, (LANES, LANES), 0)
        lane = lax.broadcasted_iota(jnp.int32, (LANES, LANES), 1)
        jx = here + TILES * lane
        kx = jnp.where(jx < NX // 2, jx, jx - NX).astype(f32) * (2 * math.pi / (NX * cell_spacing))

        @pl.loop(0, YA // 2)
        def _(k):
            for part in range(2):
                ka = 2 * k + part
                cols = slice(part * LANES, (part + 1) * LANES)
                jy = ka + YA * kb
                ky = jnp.where(jy < NY // 2, jy, jy - NY).astype(f32) * (2 * math.pi / (NY * cell_spacing))
                vertical = (omega / base_speed) ** 2 - (ky * ky + kx * kx)
                root = layer_thickness * jnp.sqrt(jnp.abs(vertical))
                damping = jnp.exp(jnp.where(vertical < 0.0, -root, 0.0)) * (1.0 / (NX * NY))
                sine, cosine = sin_cos(jnp.where(vertical > 0.0, root, 0.0))
                hcos[k, :, cols] = damping * cosine
                hsin[k, :, cols] = damping * sine

    def make_phase(step, omega):
        @pl.loop(0, ROWS // 8)
        def _(g):
            rows = pl.ds(pl.multiple_of(g * 8, 8), 8)
            for q in range(4):
                cols = slice(q * NX // 4, (q + 1) * NX // 4)
                shift = (omega * layer_thickness) * slow[step, rows, cols]
                sine, cosine = sin_cos(shift)
                phc[step, rows, cols] = cosine
                phs[step, rows, cols] = sine

    quarter = pl.ds(pl.multiple_of(x * 2 * PIECE, 2 * PIECE), 2 * PIECE)

    def velocity_start():
        @pl.loop(1, 4)
        def _(j):
            px = (x + j) % 4
            rows = pl.ds(pl.multiple_of(px * 2 * PIECE, 2 * PIECE), 2 * PIECE)
            remote(vel_ref.at[rows], vrecv.at[x], vsend.at[0], vrcv.at[0], dev(px, y, zh, zl, c)).start()

        pltpu.make_async_copy(vel_ref.at[quarter], vrecv.at[x], vloc.at[0]).start()

    def velocity_all():
        part = vrecv.at[pl.ds(0, 3)]
        return remote(part, part, vsend.at[0], vrcv.at[0], across_odd)

    partner = dev(x, y, zh, 1 - zl, c)
    own_half = pl.ds(pl.multiple_of(zl * PIECE, PIECE), PIECE)
    other_half = pl.ds(pl.multiple_of((1 - zl) * PIECE, PIECE), PIECE)
    pair0 = remote(vsel.at[0, other_half], vpart.at[0, pl.ds(0, PIECE)], vsend.at[1], vrcv.at[1], partner)
    pair1 = remote(vsel.at[1], vpart.at[1], vsend.at[2], vrcv.at[2], partner)
    turn = remote(vsel.at[2, pl.ds(0, PIECE)], vturn, vsend.at[3], vrcv.at[3], across)
    turn_here = pltpu.make_async_copy(vsel.at[2, pl.ds(0, PIECE)], vturn, vloc.at[1])

    def velocity_select():
        velocity_all().wait_recv()
        pltpu.make_async_copy(vel_ref.at[quarter], vrecv.at[x], vloc.at[0]).wait()
        for step in range(2):
            chosen = owner_ref[step]
            piece = 1.0 / vrecv[chosen // 2] - 1.0 / base_speed
            vsel[step] = jnp.where(chosen % 2 == zl, piece, 0.0)
        pair0.start()

    def velocity_turn():
        pair0.wait_recv()
        vsel[2, 0:PIECE] = vsel[0, own_half] + vpart[0, 0:PIECE]

        @pl.when(x != zh)
        def _():
            turn.start()

        @pl.when(x == zh)
        def _():
            turn_here.start()

    def velocity_spread():
        @pl.when(x != zh)
        def _():
            turn.wait_recv()

        @pl.when(x == zh)
        def _():
            turn_here.wait()

        velocity_along_z()

    eighth = pl.ds(pl.multiple_of(z * PIECE, PIECE), PIECE)

    def velocity_along_z():
        @pl.loop(1, 8)
        def _(j):
            remote(vturn, slow.at[0, eighth], vsend.at[4], vrcv.at[4], along_z(j)[0]).start()

        slow[0, eighth] = vturn[...]

    def along_z_all():
        part = slow.at[0, pl.ds(0, 7 * PIECE)]
        return remote(part, part, vsend.at[4], vrcv.at[4], across_odd)

    def velocity_along_x():
        pair1.wait_recv()
        piece = vsel[1] + vpart[1]
        vsel[3] = piece
        slow[1, quarter] = piece

        @pl.loop(1, 4)
        def _(j):
            remote(vsel.at[3], slow.at[1, quarter], vsend.at[5], vrcv.at[5], dev((x + j) % 4, y, zh, zl, c)).start()

    def along_x_all():
        part = slow.at[1, pl.ds(0, 6 * PIECE)]
        return remote(part, part, vsend.at[5], vrcv.at[5], across_odd)

    def image_start(step, ch):
        rows = chunk_rows(ch)
        mine = z if step == 0 else f

        @pl.loop(1, 8)
        def _(j):
            if step == 0:
                device, p = along_z(j)
            else:
                p = (f + j) % 8
                device = (p, me)
            cols = pl.ds(pl.multiple_of(p * BAND, BAND), BAND)
            remote(
                terms.at[step, rows, cols], irecv.at[step, mine, rows],
                isend.at[step, ch], ircv.at[step, ch], device,
            ).start()

        cols = pl.ds(pl.multiple_of(mine * BAND, BAND), BAND)
        pltpu.make_async_copy(terms.at[step, rows, cols], irecv.at[step, mine, rows], iloc.at[step, ch]).start()

    def image_all(step, ch):
        part = irecv.at[step, pl.ds(0, FREQ - 1), chunk_rows(ch)]
        return remote(part, part, isend.at[step, ch], ircv.at[step, ch], across_odd)

    def image_sum(step, ch):
        rows = chunk_rows(ch)
        image_all(step, ch).wait_recv()
        part = irecv.at[step, 0, rows]
        pltpu.make_async_copy(part, part, iloc.at[step, ch]).wait()
        total = irecv[step, 0, rows, :]
        for j in range(1, FREQ):
            total = total + irecv[step, j, rows, :]
        return rows, total

    back = remote(isum, iback, tsend.at[0], trecv.at[0], across)
    back_here = pltpu.make_async_copy(isum, iback, tloc.at[0])

    omega = 2 * math.pi * (lowest_hertz + hertz_step * fidx_ref[0].astype(f32))
    omega_out[...] = jnp.full((8, LANES), omega, f32)
    omega_turn = remote(omega_out, omega_in, tsend.at[1], trecv.at[1], across_odd)
    for ch in range(CHUNKS):
        forward_x(wave_ref.at[0, 0], wave_ref.at[0, 1], sendx.at[0], ch)
    make_twiddles()
    pl.semaphore_wait(barrier, 31 + 7 + 3 + 1 + 1)
    omega_turn.start()
    spread(sendx.at[0], recvy.at[0])
    omega_turn.wait_recv()
    omega_col = omega_in[0:1, :]
    velocity_select()
    make_tables(omega_col)
    recvy_all = remote(recvy.at[0], recvy.at[0], zsend.at[0], zrecv.at[0], across_odd)

    @pl.when(c == 1)
    def _():
        velocity_turn()

    recvy_all.wait_recv()
    pl.semaphore_signal(gate.at[1], inc=1, device_id=other_core, device_id_type=MESH)

    @pl.when(c == 1)
    def _():
        pl.semaphore_wait(gate.at[1], 1)
        velocity_spread()

    column_pass(recvy.at[0], sendy.at[0], lambda ch: a2a_start(sendy.at[0], recvx.at[0], ch, 0))


    @pl.when(c == 0)
    def _():
        velocity_turn()
        pl.semaphore_wait(gate.at[1], 1)
        velocity_spread()

    along_z_all().wait_recv()
    make_phase(0, omega_in[0:1, 0:1])
    for ch in range(CHUNKS):
        a2a_wait_recv(recvx.at[0], ch, 0)
        inverse_x(recvx.at[0], 0, terms.at[0], imag, ch)
        forward_x(terms.at[0], imag, sendx.at[1], ch)
        a2a_start_core(sendx.at[1], recvy.at[1], ch, 1, 0)
        image_start(0, ch)
    for ch in range(CHUNKS):
        a2a_core_sent(sendx.at[1], ch, 1, 0)
        a2a_start_core(sendx.at[1], recvy.at[1], ch, 1, 1)
    pair1.start()
    for ch in range(CHUNKS):
        a2a_wait_recv(recvy.at[1], ch, 1)

    def collect_first(ch):
        if ch == 0:
            @pl.loop(0, BEHIND)
            def _(i):
                collect_send(sendy.at[1], i)

    column_pass(recvy.at[1], sendy.at[1], collect_first)
    velocity_along_x()
    for ch in range(CHUNKS):
        rows, total = image_sum(0, ch)
        isum[rows, :] = total

    @pl.when(x != zh)
    def _():
        back.start()

    @pl.when(x == zh)
    def _():
        back_here.start()

    def finish(ch):
        collect_wait_recv(recvx.at[1], ch)
        inverse_x(recvx.at[1], 1, terms.at[1], field_ref.at[0, 1], ch)
        image_start(1, ch)
        rows = chunk_rows(ch)
        field_ref[0, 0, rows, :] = terms[1, rows, :]

    collect(sendy.at[1], recvx.at[1], 0, 32)
    along_x_all().wait_recv()
    make_phase(1, omega)
    for ch in range(1, CHUNKS):
        collect(sendy.at[1], recvx.at[1], 32 * ch, 32 * ch + 16)
        finish(ch - 1)
        collect(sendy.at[1], recvx.at[1], 32 * ch + 16, 32 * ch + 32)
    finish(CHUNKS - 1)

    @pl.when(x != zh)
    def _():
        back.wait()
        turn.wait_send()

    @pl.when(x == zh)
    def _():
        back_here.wait()

    image_ref[0] = iback[...]
    for ch in range(CHUNKS):
        rows, total = image_sum(1, ch)
        image_ref[1, rows, :] = total

    omega_turn.wait_send()
    recvy_all.wait_send()
    velocity_all().wait_send()
    pair0.wait_send()
    pair1.wait_send()
    along_z_all().wait_send()
    along_x_all().wait_send()
    for ch in range(CHUNKS):
        part = relay.at[1, :, chunk_rows(ch)]
        remote(part, part, zsend.at[1 + ch], rrecv.at[1 + ch, 0], across_odd).wait_send()
        collect_all(recvx.at[1], ch).wait_send()
        a2a_all(recvx.at[0], ch, 0).wait_send()
        a2a_core_sent(sendx.at[1], ch, 1, 1)
        for step in range(2):
            image_all(step, ch).wait_send()


def tables():
    n = np.arange(LANES)
    angle = 2 * np.pi * ((n[:, None] * n[None, :]) % LANES) / LANES
    c, s = np.cos(angle), np.sin(angle)
    right = np.block([[c, -s], [s, c]])
    out = []
    for m in (right, right.T):
        high = m.astype(ml_dtypes.bfloat16)
        out += [high, (m - high.astype(np.float64)).astype(ml_dtypes.bfloat16)]
    out += [np.concatenate(out[:2]), np.concatenate(out[2:4])]
    tx = 2 * np.pi * ((np.arange(TILES)[:, None] * n[None, :]) % NX) / NX
    return [np.cos(tx).astype(np.float32), np.sin(tx).astype(np.float32)] + out


def hand_kernel(image_in, field_in, image_out, field_out):
    image_out[...] = image_in[...]
    field_out[...] = field_in[...]


def hand_over(image, field):
    specs = (
        pl.BlockSpec((2, ROWS // 4, BAND), lambda i: (0, i, 0)),
        pl.BlockSpec((1, 2, ROWS // 4, NX), lambda i: (0, 0, i, 0)),
    )
    return pl.pallas_call(
        hand_kernel,
        grid=(4,),
        out_shape=(
            jax.ShapeDtypeStruct(image.shape, f32),
            jax.ShapeDtypeStruct(field.shape, f32),
        ),
        in_specs=specs,
        out_specs=specs,
        name="hand_over",
    )(image, field)


def shards(wavefield, velocity, freq_index, owner):
    vmem = pl.BlockSpec(memory_space=pltpu.VMEM)
    smem = pl.BlockSpec(memory_space=pltpu.SMEM)
    dma = pltpu.SemaphoreType.DMA
    big = (SPACE, ROWS, 2 * LANES)
    image, field = pl.pallas_call(
        kernel,
        out_shape=(
            jax.ShapeDtypeStruct((2, ROWS, BAND), f32),
            jax.ShapeDtypeStruct((1, 2, ROWS, NX), f32),
        ),
        in_specs=[smem, smem] + [vmem] * 10,
        out_specs=(vmem, vmem),
        scratch_shapes=[
            pltpu.VMEM((TILES, CHUNK, 2 * LANES), f32),
            pltpu.VMEM((2,) + big, f32),
            pltpu.VMEM((2,) + big, f32),
            pltpu.VMEM((2,) + big, f32),
            pltpu.VMEM((2,) + big, f32),
            pltpu.VMEM((2,) + big, f32),
            pltpu.VMEM((YA // 2, 2 * LANES, 2 * LANES), f32),
            pltpu.VMEM((YA // 2, LANES, 2 * LANES), f32),
            pltpu.VMEM((YA // 2, LANES, 2 * LANES), f32),
            pltpu.VMEM((YA // 2, LANES, 2 * LANES), f32),
            pltpu.VMEM((YA // 2, LANES, 2 * LANES), f32),
            pltpu.VMEM((4, 2 * PIECE, NX), f32),
            pltpu.VMEM((4, 2 * PIECE, NX), f32),
            pltpu.VMEM((2, 2 * PIECE, NX), f32),
            pltpu.VMEM((PIECE, NX), f32),
            pltpu.VMEM((2, ROWS, NX), f32),
            pltpu.VMEM((2, ROWS, NX), f32),
            pltpu.VMEM((2, ROWS, NX), f32),
            pltpu.VMEM((2, ROWS, NX), f32),
            pltpu.VMEM((ROWS, NX), f32),
            pltpu.VMEM((2, FREQ, ROWS, BAND), f32),
            pltpu.VMEM((ROWS, BAND), f32),
            pltpu.VMEM((ROWS, BAND), f32),
            pltpu.VMEM((8, LANES), f32),
            pltpu.VMEM((8, LANES), f32),
            dma((2, CHUNKS)), dma((2, CHUNKS)), dma((2, CHUNKS)),
            dma((1 + CHUNKS,)), dma((1 + CHUNKS, 32)), dma((1 + CHUNKS,)), dma((1 + CHUNKS,)), dma((CHUNKS,)),
            dma((6,)), dma((6,)), dma((2,)),
            dma((2, CHUNKS)), dma((2, CHUNKS)), dma((2, CHUNKS)),
            dma((2,)), dma((2,)), dma((1,)), pltpu.SemaphoreType.REGULAR((2,)), dma((2, CHUNKS)), dma((32,)),
        ],
        compiler_params=pltpu.CompilerParams(
            collective_id=0, has_side_effects=True, vmem_limit_bytes=60 * 2**20
        ),
        name="migrate",
    )(freq_index, owner, wavefield, velocity[0], *tables())
    return hand_over(image, field)


def solution(mesh):
    return jax.shard_map(
        shards,
        mesh=mesh,
        in_specs=(P("freq", None, "space", None), P("freq", "space", None), P("freq"), P()),
        out_specs=(P(None, "space", "freq"), P("freq", None, "space", None)),
        check_vma=False,
    )
```

```python
import functools
import math

import jax
import jax.numpy as jnp
import ml_dtypes
import numpy as np
from jax import lax
from jax.experimental import pallas as pl
from jax.experimental.pallas import tpu as pltpu
from jax.sharding import PartitionSpec as P

NX, NY = 4096, 2048
SPACE, FREQ = 32, 8
ROWS = NY // SPACE
LANES = 128
TILES = NX // LANES
YA = NY // LANES
CHUNK = 32
CHUNKS = ROWS // CHUNK
BAND = NX // FREQ
PIECE = ROWS // FREQ
AHEAD, BEHIND, WINDOW = 16, 16, 16

cell_spacing = 25.0
layer_thickness = 10.0
base_speed = 1500.0
lowest_hertz = 5.0
hertz_step = 0.9
MESH = pl.DeviceIdType.MESH
f32 = jnp.float32
bf16 = jnp.bfloat16


def times_root(value, power, length, sign):
    re, im = value
    power = power % length
    quarter = 4 * power
    if quarter % length == 0:
        turn = quarter // length
        if sign < 0:
            turn = (4 - turn) % 4
        return [(re, im), (-im, re), (-re, -im), (im, -re)][turn]
    angle = sign * 2 * math.pi * power / length
    c, s = math.cos(angle), math.sin(angle)
    if (8 * power) % length == 0:
        h = math.sqrt(0.5)
        cs, ss = math.copysign(1, c), math.copysign(1, s)
        p, q = re * h, im * h
        real = (p if cs > 0 else -p) + (-q if ss > 0 else q)
        imag = (p if ss > 0 else -p) + (q if cs > 0 else -q)
        return (real, imag)
    return (re * c - im * s, re * s + im * c)


def add(a, b):
    return (a[0] + b[0], a[1] + b[1])


def sub(a, b):
    return (a[0] - b[0], a[1] - b[1])


def small_dft(values, sign):
    n = len(values)
    if n == 1:
        return values
    if n == 2:
        return [add(values[0], values[1]), sub(values[0], values[1])]
    m = n // 4
    parts = [small_dft(values[r::4], sign) for r in range(4)]
    out = [None] * n
    for k in range(m):
        a = parts[0][k]
        b, c, d = (times_root(parts[r][k], r * k, n, sign) for r in (1, 2, 3))
        s0, s1 = add(a, c), sub(a, c)
        s2, s3 = add(b, d), times_root(sub(b, d), 1, 4, sign)
        out[k], out[k + m] = add(s0, s2), add(s1, s3)
        out[k + 2 * m], out[k + 3 * m] = sub(s0, s2), sub(s1, s3)
    return out


def sin_cos(t):
    n = jnp.floor(t * (2 / math.pi) + 0.5)
    r = (t - n * 1.5703125) - n * 4.83826794896e-4
    z = r * r
    s = r + r * z * (-1.6666654611e-1 + z * (8.3321608736e-3 + z * -1.9515295891e-4))
    c = 1.0 - 0.5 * z + z * z * (4.166664568298827e-2 + z * (-1.388731625493765e-3 + z * 2.443315711809948e-5))
    half = n * 0.5
    odd = half != jnp.floor(half)
    quad = n - 4.0 * jnp.floor(n * 0.25)
    sine = jnp.where(odd, c, s)
    cosine = jnp.where(odd, s, c)
    sine = jnp.where(quad >= 2.0, -sine, sine)
    cosine = jnp.where((quad == 1.0) | (quad == 2.0), -cosine, cosine)
    return sine, cosine


def split(value):
    high = value.astype(bf16)
    return high, (value - high.astype(f32)).astype(bf16)


def mul3(a, b):
    ah, al = a
    bh, bl = b
    dot = functools.partial(jnp.dot, preferred_element_type=f32)
    return dot(ah, bh) + (dot(al, bh) + dot(ah, bl))


def left_mul3(left_ref, b):
    bh, bl = b
    n = bh.shape[0]
    dot = functools.partial(jnp.dot, preferred_element_type=f32)
    both = dot(left_ref[...], bh)
    return both[:n] + (both[n:] + dot(left_ref[:n, :], bl))


def kernel(
    fidx_ref, owner_ref, wave_ref, vel_ref, txc_ref, txs_ref, rh_ref, rl_ref, lh_ref, ll_ref, rs_ref, ls_ref,
    image_ref, field_ref,
    rowbuf, sendx, sendy, recvy, recvx, relay, mid, hcos, hsin, tyc, tys,
    vrecv, vsel, vpart, vturn, slow, phc, phs, terms, imag, irecv, isum, iback, omega_out, omega_in,
    asend, arecv, aloc, rsend, rrecv, zsend, zrecv, rloc,
    vsend, vrcv, vloc, isend, ircv, iloc, tsend, trecv, tloc, gate, gsend, grecv, csend, psend,
):
    f = lax.axis_index("freq")
    me = lax.axis_index("space")
    x, zl = f // 2, f % 2
    zh, y, c = me // 8, (me // 2) % 4, me % 2
    z = zh * 2 + zl
    here = (x * 4 + y) * 2 + c

    def dev(dx, dy, dzh, dzl, dc):
        return (dx * 2 + dzl, (dzh * 4 + dy) * 2 + dc)

    def plane(j):
        px, py, pc = (x + j % 4) % 4, (y + j // 4 + j) % 4, (c + j // 16) % 2
        return dev(px, py, zh, zl, pc), (px * 4 + py) * 2 + pc

    def along_z(j):
        pz = (z + j) % 8
        return dev(x, y, pz // 2, pz % 2, c), pz

    other_core = dev(x, y, zh, zl, 1 - c)
    across = dev(zh, y, x, zl, c)
    across_odd = dev(zh, y, x, 1 - zl, c)

    barrier = pltpu.get_barrier_semaphore()

    def greet(device):
        pl.semaphore_signal(barrier, inc=1, device_id=device, device_id_type=MESH)

    @pl.loop(1, 32)
    def _(j):
        greet(plane(j)[0])

    @pl.loop(1, 8)
    def _(j):
        greet(along_z(j)[0])

    @pl.loop(1, 4)
    def _(j):
        greet(dev((x + j) % 4, y, zh, 1 - zl, c))

    greet(across_odd)

    @pl.when(x != zh)
    def _():
        greet(across)

    @pl.when(x == zh)
    def _():
        greet(across_odd)

    def remote(src, dst, send, recv, device):
        return pltpu.make_async_remote_copy(
            src_ref=src, dst_ref=dst, send_sem=send, recv_sem=recv, device_id=device, device_id_type=MESH
        )

    def chunk_rows(ch):
        return pl.ds(ch * CHUNK, CHUNK)

    def a2a_start(src, dst, ch, i):
        rows = chunk_rows(ch)

        @pl.loop(1, 32)
        def _(j):
            device, place = plane(j)
            remote(src.at[place, rows], dst.at[here, rows], asend.at[i, ch], arecv.at[i, ch], device).start()

        pltpu.make_async_copy(src.at[here, rows], dst.at[here, rows], aloc.at[i, ch]).start()

    def a2a_start_core(src, dst, ch, i, core):
        rows = chunk_rows(ch)

        @pl.loop(0, 16)
        def _(k):
            px, py = (x + k % 4) % 4, (y + k // 4 + k) % 4
            place = (px * 4 + py) * 2 + core

            @pl.when(place != here)
            def _():
                remote(
                    src.at[place, rows], dst.at[here, rows], csend.at[core, ch], arecv.at[i, ch],
                    dev(px, py, zh, zl, core),
                ).start()

            @pl.when(place == here)
            def _():
                pltpu.make_async_copy(src.at[here, rows], dst.at[here, rows], aloc.at[i, ch]).start()

    def a2a_core_sent(dst, ch, i, core):
        @pl.when(c == core)
        def _():
            part = dst.at[pl.ds(0, 15), chunk_rows(ch)]
            remote(part, part, csend.at[core, ch], arecv.at[i, ch], across_odd).wait_send()

        @pl.when(c != core)
        def _():
            part = dst.at[pl.ds(0, 16), chunk_rows(ch)]
            remote(part, part, csend.at[core, ch], arecv.at[i, ch], across_odd).wait_send()

    def a2a_all(dst, ch, i):
        part = dst.at[pl.ds(0, SPACE - 1), chunk_rows(ch)]
        return remote(part, part, asend.at[i, ch], arecv.at[i, ch], across_odd)

    def a2a_wait_recv(dst, ch, i):
        a2a_all(dst, ch, i).wait_recv()
        part = dst.at[here, chunk_rows(ch)]
        pltpu.make_async_copy(part, part, aloc.at[i, ch]).wait()

    def spread_send(src, q, sent=False):
        k, pc = q % 16, q // 16
        px, py = (x + k + zh) % 4, (y + k // 4 + k) % 4
        place, slot = (px * 4 + py) * 2 + pc, k * 2 + c

        @pl.when(place != here)
        def _():
            copy = remote(
                src.at[place], relay.at[0, slot], psend.at[q], rrecv.at[0, slot], dev(px, py, zh, zl, pc)
            )
            if sent:
                copy.wait_send()
            else:
                copy.start()

    def spread_relay(src, dst, r):
        k, pc = r // 2, r % 2
        px, py = (x + 64 - k - zh) % 4, (y + 64 - k // 4 - k) % 4
        place, slot = (px * 4 + py) * 2 + pc, (zh * 4 + py) * 2 + pc
        target = dev(x, y, px, 1 - zl, c)

        @pl.when(place == here)
        def _():
            remote(src.at[here], dst.at[slot], zsend.at[0], zrecv.at[0], target).start()

        @pl.when(place != here)
        def _():
            remote(relay.at[0, r], relay.at[0, r], rsend.at[0], rrecv.at[0, r], across_odd).wait_recv()
            remote(relay.at[0, r], dst.at[slot], zsend.at[0], zrecv.at[0], target).start()

    def spread(src, dst):
        ahead = AHEAD + (32 - AHEAD) * c

        @pl.loop(0, ahead)
        def _(q):
            @pl.when(q >= WINDOW)
            def _():
                spread_send(src, q - WINDOW, True)

            spread_send(src, q)

        @pl.when(c == 1)
        def _():
            @pl.loop(32 - WINDOW, 32)
            def _(q):
                spread_send(src, q, True)

            velocity_start()
            pl.semaphore_wait(gate.at[0], 1)

        @pl.loop(0, 32)
        def _(r):
            spread_relay(src, dst, r)

            @pl.when((c == 0) & (r == 12))
            def _():
                velocity_start()

            @pl.when(ahead + r < 32)
            def _():
                spread_send(src, ahead + r - WINDOW, True)
                spread_send(src, ahead + r)

        @pl.when(c == 0)
        def _():
            @pl.loop(32 - WINDOW, 32)
            def _(q):
                spread_send(src, q, True)

            pl.semaphore_signal(gate.at[0], inc=1, device_id=other_core, device_id_type=MESH)

    def collect_send(src, i):
        ch, j = i // 32, i % 32
        rows = pl.ds(pl.multiple_of(ch * CHUNK, CHUNK), CHUNK)
        pzh, py, pc = (zh + j + x) % 4, (y + j // 8) % 4, (c + (j // 4) % 2) % 2
        remote(
            src.at[(pzh * 4 + py) * 2 + pc, rows], relay.at[1, j, rows],
            zsend.at[1 + ch], rrecv.at[1 + ch, j], dev(x, y, pzh, 1 - zl, c),
        ).start()

    def collect_relay(dst, i):
        ch, j = i // 32, i % 32
        rows = pl.ds(pl.multiple_of(ch * CHUNK, CHUNK), CHUNK)
        px, py, pc = (zh + 64 - j - x) % 4, (y + j // 8) % 4, (c + (j // 4) % 2) % 2
        place = (px * 4 + py) * 2 + pc
        part = relay.at[1, j, rows]
        remote(part, part, zsend.at[1 + ch], rrecv.at[1 + ch, j], across_odd).wait_recv()

        @pl.when(place == here)
        def _():
            pltpu.make_async_copy(part, dst.at[here, rows], rloc.at[ch]).start()

        @pl.when(place != here)
        def _():
            remote(part, dst.at[here, rows], rsend.at[1 + ch], zrecv.at[1 + ch], dev(px, py, zh, zl, pc)).start()

    def collect(src, dst, low, high):
        @pl.loop(low, high)
        def _(i):
            collect_relay(dst, i)

            @pl.when(BEHIND + i < 32 * CHUNKS)
            def _():
                collect_send(src, BEHIND + i)

    def collect_all(dst, ch):
        part = dst.at[pl.ds(0, SPACE - 1), chunk_rows(ch)]
        return remote(part, part, rsend.at[1 + ch], zrecv.at[1 + ch], across_odd)

    def collect_wait_recv(dst, ch):
        collect_all(dst, ch).wait_recv()
        part = dst.at[here, chunk_rows(ch)]
        pltpu.make_async_copy(part, part, rloc.at[ch]).wait()

    def forward_x(re_ref, im_ref, dst, ch):
        @pl.loop(0, CHUNK // 8)
        def _(g):
            rows = pl.ds(pl.multiple_of(ch * CHUNK + g * 8, 8), 8)
            local = pl.ds(pl.multiple_of(g * 8, 8), 8)
            vals = [
                (re_ref[rows, a * LANES:(a + 1) * LANES], im_ref[rows, a * LANES:(a + 1) * LANES])
                for a in range(TILES)
            ]
            vals = small_dft(vals, -1)
            for k in range(TILES):
                re, im = vals[k]
                c, s = txc_ref[k:k + 1, :], txs_ref[k:k + 1, :]
                rowbuf[k, local, 0:LANES] = re * c + im * s
                rowbuf[k, local, LANES:] = im * c - re * s

        @pl.loop(0, TILES // 8)
        def _(g):
            some = pl.ds(g * 8, 8)
            block = rowbuf[some].reshape(8 * CHUNK, 2 * LANES)
            out = mul3(split(block), (rh_ref[...], rl_ref[...]))
            dst[some, pl.ds(ch * CHUNK, CHUNK), :] = out.reshape(8, CHUNK, 2 * LANES)

    def inverse_x(src, step, re_ref, im_ref, ch):
        @pl.loop(0, TILES // 8)
        def _(g):
            some = pl.ds(g * 8, 8)
            block = src[some, pl.ds(ch * CHUNK, CHUNK), :].reshape(8 * CHUNK, 2 * LANES)
            out = mul3(split(block), (lh_ref[...], ll_ref[...]))
            rowbuf[some] = out.reshape(8, CHUNK, 2 * LANES)

        @pl.loop(0, CHUNK // 8)
        def _(g):
            rows = pl.ds(pl.multiple_of(ch * CHUNK + g * 8, 8), 8)
            local = pl.ds(pl.multiple_of(g * 8, 8), 8)
            vals = []
            for k in range(TILES):
                re, im = rowbuf[k, local, 0:LANES], rowbuf[k, local, LANES:]
                c, s = txc_ref[k:k + 1, :], txs_ref[k:k + 1, :]
                vals.append((re * c - im * s, im * c + re * s))
            vals = small_dft(vals, 1)
            for a in range(TILES):
                re, im = vals[a]
                cols = slice(a * LANES, (a + 1) * LANES)
                c, s = phc[step, rows, cols], phs[step, rows, cols]
                re_ref[rows, cols] = re * c - im * s
                im_ref[rows, cols] = re * s + im * c

    def column_pass(src, dst, send):
        @pl.loop(0, LANES // 8)
        def _(t):
            half, sub_rows = t // 8, pl.ds(pl.multiple_of(t % 8 * 8, 8), 8)
            vals = [
                (src[2 * a + half, sub_rows, 0:LANES], src[2 * a + half, sub_rows, LANES:]) for a in range(YA)
            ]
            vals = small_dft(vals, -1)
            re_rows = pl.ds(pl.multiple_of(t * 8, 8), 8)
            im_rows = pl.ds(pl.multiple_of(LANES + t * 8, 8), 8)
            for k in range(YA):
                re, im = vals[k]
                cols = slice(k % 2 * LANES, k % 2 * LANES + LANES)
                c, s = tyc[k // 2, re_rows, cols], tys[k // 2, re_rows, cols]
                mid[k // 2, re_rows, cols] = re * c + im * s
                mid[k // 2, im_rows, cols] = im * c - re * s

        @pl.loop(0, YA // 2)
        def _(k):
            spec = left_mul3(ls_ref, split(mid[k]))
            re, im = spec[:LANES], spec[LANES:]
            c, s = hcos[k], hsin[k]
            spec = jnp.concatenate([re * c - im * s, re * s + im * c], axis=0)
            mid[k] = left_mul3(rs_ref, split(spec))

        for ch in range(CHUNKS):
            @pl.loop(0, CHUNK // 4)
            def _(q):
                half, tile = q % 2, ch * (CHUNK // 8) + q // 2
                t = half * 8 + tile
                re_rows = pl.ds(pl.multiple_of(t * 8, 8), 8)
                im_rows = pl.ds(pl.multiple_of(LANES + t * 8, 8), 8)
                vals = []
                for k in range(YA):
                    cols = slice(k % 2 * LANES, k % 2 * LANES + LANES)
                    re, im = mid[k // 2, re_rows, cols], mid[k // 2, im_rows, cols]
                    c, s = tyc[k // 2, re_rows, cols], tys[k // 2, re_rows, cols]
                    vals.append((re * c - im * s, im * c + re * s))
                vals = small_dft(vals, 1)
                out_rows = pl.ds(pl.multiple_of(tile * 8, 8), 8)
                for a in range(YA):
                    dst[2 * a + half, out_rows, 0:LANES] = vals[a][0]
                    dst[2 * a + half, out_rows, LANES:] = vals[a][1]
            send(ch)

    def make_twiddles():
        kb = lax.broadcasted_iota(jnp.int32, (LANES, LANES), 0)

        @pl.loop(0, YA // 2)
        def _(k):
            for part in range(2):
                cols = slice(part * LANES, (part + 1) * LANES)
                sine, cosine = sin_cos(((2 * k + part) * kb).astype(f32) * (2 * math.pi / NY))
                tyc[k, :, cols] = cosine
                tys[k, :, cols] = sine

    def make_tables(omega):
        kb = lax.broadcasted_iota(jnp.int32, (LANES, LANES), 0)
        lane = lax.broadcasted_iota(jnp.int32, (LANES, LANES), 1)
        jx = here + TILES * lane
        kx = jnp.where(jx < NX // 2, jx, jx - NX).astype(f32) * (2 * math.pi / (NX * cell_spacing))

        @pl.loop(0, YA // 2)
        def _(k):
            for part in range(2):
                ka = 2 * k + part
                cols = slice(part * LANES, (part + 1) * LANES)
                jy = ka + YA * kb
                ky = jnp.where(jy < NY // 2, jy, jy - NY).astype(f32) * (2 * math.pi / (NY * cell_spacing))
                vertical = (omega / base_speed) ** 2 - (ky * ky + kx * kx)
                root = layer_thickness * jnp.sqrt(jnp.abs(vertical))
                damping = jnp.exp(jnp.where(vertical < 0.0, -root, 0.0)) * (1.0 / (NX * NY))
                sine, cosine = sin_cos(jnp.where(vertical > 0.0, root, 0.0))
                hcos[k, :, cols] = damping * cosine
                hsin[k, :, cols] = damping * sine

    def make_phase(step, omega):
        @pl.loop(0, ROWS // 8)
        def _(g):
            rows = pl.ds(pl.multiple_of(g * 8, 8), 8)
            for q in range(4):
                cols = slice(q * NX // 4, (q + 1) * NX // 4)
                shift = (omega * layer_thickness) * slow[step, rows, cols]
                sine, cosine = sin_cos(shift)
                phc[step, rows, cols] = cosine
                phs[step, rows, cols] = sine

    quarter = pl.ds(pl.multiple_of(x * 2 * PIECE, 2 * PIECE), 2 * PIECE)

    def velocity_start():
        @pl.loop(1, 4)
        def _(j):
            px = (x + j) % 4
            rows = pl.ds(pl.multiple_of(px * 2 * PIECE, 2 * PIECE), 2 * PIECE)
            remote(vel_ref.at[rows], vrecv.at[x], vsend.at[0], vrcv.at[0], dev(px, y, zh, zl, c)).start()

        pltpu.make_async_copy(vel_ref.at[quarter], vrecv.at[x], vloc.at[0]).start()

    def velocity_all():
        part = vrecv.at[pl.ds(0, 3)]
        return remote(part, part, vsend.at[0], vrcv.at[0], across_odd)

    partner = dev(x, y, zh, 1 - zl, c)
    own_half = pl.ds(pl.multiple_of(zl * PIECE, PIECE), PIECE)
    other_half = pl.ds(pl.multiple_of((1 - zl) * PIECE, PIECE), PIECE)
    pair0 = remote(vsel.at[0, other_half], vpart.at[0, pl.ds(0, PIECE)], vsend.at[1], vrcv.at[1], partner)
    pair1 = remote(vsel.at[1], vpart.at[1], vsend.at[2], vrcv.at[2], partner)
    turn = remote(vsel.at[2, pl.ds(0, PIECE)], vturn, vsend.at[3], vrcv.at[3], across)
    turn_here = pltpu.make_async_copy(vsel.at[2, pl.ds(0, PIECE)], vturn, vloc.at[1])

    def velocity_select():
        velocity_all().wait_recv()
        pltpu.make_async_copy(vel_ref.at[quarter], vrecv.at[x], vloc.at[0]).wait()
        for step in range(2):
            chosen = owner_ref[step]
            piece = 1.0 / vrecv[chosen // 2] - 1.0 / base_speed
            vsel[step] = jnp.where(chosen % 2 == zl, piece, 0.0)
        pair0.start()

    def velocity_turn():
        pair0.wait_recv()
        vsel[2, 0:PIECE] = vsel[0, own_half] + vpart[0, 0:PIECE]

        @pl.when(x != zh)
        def _():
            turn.start()

        @pl.when(x == zh)
        def _():
            turn_here.start()

    def velocity_spread():
        @pl.when(x != zh)
        def _():
            turn.wait_recv()

        @pl.when(x == zh)
        def _():
            turn_here.wait()

        velocity_along_z()

    eighth = pl.ds(pl.multiple_of(z * PIECE, PIECE), PIECE)

    def ring_copy(k):
        offset = (2, -2, 1, -1, 1, -1, 2, -2)[k]
        source = (0, 0, 0, 0, -2, 2, -2, 2)[k]
        cols = (slice(0, NX // 2) if k == 6 else slice(NX // 2, NX)) if k >= 6 else slice(0, NX)
        rows = pl.ds(pl.multiple_of((z + 8 + source) % 8 * PIECE, PIECE), PIECE)
        part = slow.at[0, rows, cols]
        return remote(part, part, gsend.at[k], grecv.at[k], along_z((8 + offset) % 8)[0])

    def velocity_along_z():
        slow[0, eighth] = vturn[...]
        for k in range(4):
            ring_copy(k).start()

    def velocity_forward():
        ring_copy(0).wait_recv()
        ring_copy(1).wait_recv()
        for k in range(4, 8):
            ring_copy(k).start()
        for k in range(2, 8):
            ring_copy(k).wait_recv()

    def velocity_along_x():
        pair1.wait_recv()
        piece = vsel[1] + vpart[1]
        vsel[3] = piece
        slow[1, quarter] = piece

        @pl.loop(1, 4)
        def _(j):
            remote(vsel.at[3], slow.at[1, quarter], vsend.at[5], vrcv.at[5], dev((x + j) % 4, y, zh, zl, c)).start()

    def along_x_all():
        part = slow.at[1, pl.ds(0, 6 * PIECE)]
        return remote(part, part, vsend.at[5], vrcv.at[5], across_odd)

    def image_start(step, ch):
        rows = chunk_rows(ch)
        mine = z if step == 0 else f

        @pl.loop(1, 8)
        def _(j):
            if step == 0:
                device, p = along_z(j)
            else:
                p = (f + j) % 8
                device = (p, me)
            cols = pl.ds(pl.multiple_of(p * BAND, BAND), BAND)
            remote(
                terms.at[step, rows, cols], irecv.at[step, mine, rows],
                isend.at[step, ch], ircv.at[step, ch], device,
            ).start()

        cols = pl.ds(pl.multiple_of(mine * BAND, BAND), BAND)
        pltpu.make_async_copy(terms.at[step, rows, cols], irecv.at[step, mine, rows], iloc.at[step, ch]).start()

    def image_all(step, ch):
        part = irecv.at[step, pl.ds(0, FREQ - 1), chunk_rows(ch)]
        return remote(part, part, isend.at[step, ch], ircv.at[step, ch], across_odd)

    def image_sum(step, ch):
        rows = chunk_rows(ch)
        image_all(step, ch).wait_recv()
        part = irecv.at[step, 0, rows]
        pltpu.make_async_copy(part, part, iloc.at[step, ch]).wait()
        total = irecv[step, 0, rows, :]
        for j in range(1, FREQ):
            total = total + irecv[step, j, rows, :]
        return rows, total

    back = remote(isum, iback, tsend.at[0], trecv.at[0], across)
    back_here = pltpu.make_async_copy(isum, iback, tloc.at[0])

    omega = 2 * math.pi * (lowest_hertz + hertz_step * fidx_ref[0].astype(f32))
    omega_out[...] = jnp.full((8, LANES), omega, f32)
    omega_turn = remote(omega_out, omega_in, tsend.at[1], trecv.at[1], across_odd)
    for ch in range(CHUNKS):
        forward_x(wave_ref.at[0, 0], wave_ref.at[0, 1], sendx.at[0], ch)
    make_twiddles()
    pl.semaphore_wait(barrier, 31 + 7 + 3 + 1 + 1)
    omega_turn.start()
    spread(sendx.at[0], recvy.at[0])
    omega_turn.wait_recv()
    omega_col = omega_in[0:1, :]
    velocity_select()
    make_tables(omega_col)
    recvy_all = remote(recvy.at[0], recvy.at[0], zsend.at[0], zrecv.at[0], across_odd)

    @pl.when(c == 1)
    def _():
        velocity_turn()

    recvy_all.wait_recv()
    pl.semaphore_signal(gate.at[1], inc=1, device_id=other_core, device_id_type=MESH)

    @pl.when(c == 1)
    def _():
        pl.semaphore_wait(gate.at[1], 1)
        velocity_spread()

    column_pass(recvy.at[0], sendy.at[0], lambda ch: a2a_start(sendy.at[0], recvx.at[0], ch, 0))


    @pl.when(c == 0)
    def _():
        velocity_turn()
        pl.semaphore_wait(gate.at[1], 1)
        velocity_spread()

    velocity_forward()
    make_phase(0, omega_in[0:1, 0:1])
    for ch in range(CHUNKS):
        a2a_wait_recv(recvx.at[0], ch, 0)
        inverse_x(recvx.at[0], 0, terms.at[0], imag, ch)
        forward_x(terms.at[0], imag, sendx.at[1], ch)
        a2a_start_core(sendx.at[1], recvy.at[1], ch, 1, 0)
        image_start(0, ch)
    for ch in range(CHUNKS):
        a2a_core_sent(sendx.at[1], ch, 1, 0)
        a2a_start_core(sendx.at[1], recvy.at[1], ch, 1, 1)
    pair1.start()
    for ch in range(CHUNKS):
        a2a_wait_recv(recvy.at[1], ch, 1)

    def collect_first(ch):
        if ch == 0:
            @pl.loop(0, BEHIND)
            def _(i):
                collect_send(sendy.at[1], i)

    column_pass(recvy.at[1], sendy.at[1], collect_first)
    velocity_along_x()
    for ch in range(CHUNKS):
        rows, total = image_sum(0, ch)
        isum[rows, :] = total

    @pl.when(x != zh)
    def _():
        back.start()

    @pl.when(x == zh)
    def _():
        back_here.start()

    def finish(ch):
        collect_wait_recv(recvx.at[1], ch)
        inverse_x(recvx.at[1], 1, terms.at[1], field_ref.at[0, 1], ch)
        image_start(1, ch)
        rows = chunk_rows(ch)
        field_ref[0, 0, rows, :] = terms[1, rows, :]

    collect(sendy.at[1], recvx.at[1], 0, 32)
    along_x_all().wait_recv()
    make_phase(1, omega)
    for ch in range(1, CHUNKS):
        collect(sendy.at[1], recvx.at[1], 32 * ch, 32 * ch + 16)
        finish(ch - 1)
        collect(sendy.at[1], recvx.at[1], 32 * ch + 16, 32 * ch + 32)
    finish(CHUNKS - 1)

    @pl.when(x != zh)
    def _():
        back.wait()
        turn.wait_send()

    @pl.when(x == zh)
    def _():
        back_here.wait()

    image_ref[0] = iback[...]
    for ch in range(CHUNKS):
        rows, total = image_sum(1, ch)
        image_ref[1, rows, :] = total

    omega_turn.wait_send()
    recvy_all.wait_send()
    velocity_all().wait_send()
    pair0.wait_send()
    pair1.wait_send()
    for k in range(8):
        ring_copy(k).wait_send()
    along_x_all().wait_send()
    for ch in range(CHUNKS):
        part = relay.at[1, :, chunk_rows(ch)]
        remote(part, part, zsend.at[1 + ch], rrecv.at[1 + ch, 0], across_odd).wait_send()
        collect_all(recvx.at[1], ch).wait_send()
        a2a_all(recvx.at[0], ch, 0).wait_send()
        a2a_core_sent(sendx.at[1], ch, 1, 1)
        for step in range(2):
            image_all(step, ch).wait_send()


def tables():
    n = np.arange(LANES)
    angle = 2 * np.pi * ((n[:, None] * n[None, :]) % LANES) / LANES
    c, s = np.cos(angle), np.sin(angle)
    right = np.block([[c, -s], [s, c]])
    out = []
    for m in (right, right.T):
        high = m.astype(ml_dtypes.bfloat16)
        out += [high, (m - high.astype(np.float64)).astype(ml_dtypes.bfloat16)]
    out += [np.concatenate(out[:2]), np.concatenate(out[2:4])]
    tx = 2 * np.pi * ((np.arange(TILES)[:, None] * n[None, :]) % NX) / NX
    return [np.cos(tx).astype(np.float32), np.sin(tx).astype(np.float32)] + out


def hand_kernel(image_in, field_in, image_out, field_out):
    image_out[...] = image_in[...]
    field_out[...] = field_in[...]


def hand_over(image, field):
    specs = (
        pl.BlockSpec((2, ROWS // 4, BAND), lambda i: (0, i, 0)),
        pl.BlockSpec((1, 2, ROWS // 4, NX), lambda i: (0, 0, i, 0)),
    )
    return pl.pallas_call(
        hand_kernel,
        grid=(4,),
        out_shape=(
            jax.ShapeDtypeStruct(image.shape, f32),
            jax.ShapeDtypeStruct(field.shape, f32),
        ),
        in_specs=specs,
        out_specs=specs,
        name="hand_over",
    )(image, field)


def shards(wavefield, velocity, freq_index, owner):
    vmem = pl.BlockSpec(memory_space=pltpu.VMEM)
    smem = pl.BlockSpec(memory_space=pltpu.SMEM)
    dma = pltpu.SemaphoreType.DMA
    big = (SPACE, ROWS, 2 * LANES)
    image, field = pl.pallas_call(
        kernel,
        out_shape=(
            jax.ShapeDtypeStruct((2, ROWS, BAND), f32),
            jax.ShapeDtypeStruct((1, 2, ROWS, NX), f32),
        ),
        in_specs=[smem, smem] + [vmem] * 10,
        out_specs=(vmem, vmem),
        scratch_shapes=[
            pltpu.VMEM((TILES, CHUNK, 2 * LANES), f32),
            pltpu.VMEM((2,) + big, f32),
            pltpu.VMEM((2,) + big, f32),
            pltpu.VMEM((2,) + big, f32),
            pltpu.VMEM((2,) + big, f32),
            pltpu.VMEM((2,) + big, f32),
            pltpu.VMEM((YA // 2, 2 * LANES, 2 * LANES), f32),
            pltpu.VMEM((YA // 2, LANES, 2 * LANES), f32),
            pltpu.VMEM((YA // 2, LANES, 2 * LANES), f32),
            pltpu.VMEM((YA // 2, LANES, 2 * LANES), f32),
            pltpu.VMEM((YA // 2, LANES, 2 * LANES), f32),
            pltpu.VMEM((4, 2 * PIECE, NX), f32),
            pltpu.VMEM((4, 2 * PIECE, NX), f32),
            pltpu.VMEM((2, 2 * PIECE, NX), f32),
            pltpu.VMEM((PIECE, NX), f32),
            pltpu.VMEM((2, ROWS, NX), f32),
            pltpu.VMEM((2, ROWS, NX), f32),
            pltpu.VMEM((2, ROWS, NX), f32),
            pltpu.VMEM((2, ROWS, NX), f32),
            pltpu.VMEM((ROWS, NX), f32),
            pltpu.VMEM((2, FREQ, ROWS, BAND), f32),
            pltpu.VMEM((ROWS, BAND), f32),
            pltpu.VMEM((ROWS, BAND), f32),
            pltpu.VMEM((8, LANES), f32),
            pltpu.VMEM((8, LANES), f32),
            dma((2, CHUNKS)), dma((2, CHUNKS)), dma((2, CHUNKS)),
            dma((1 + CHUNKS,)), dma((1 + CHUNKS, 32)), dma((1 + CHUNKS,)), dma((1 + CHUNKS,)), dma((CHUNKS,)),
            dma((6,)), dma((6,)), dma((2,)),
            dma((2, CHUNKS)), dma((2, CHUNKS)), dma((2, CHUNKS)),
            dma((2,)), dma((2,)), dma((1,)), pltpu.SemaphoreType.REGULAR((2,)), dma((8,)), dma((8,)), dma((2, CHUNKS)), dma((32,)),
        ],
        compiler_params=pltpu.CompilerParams(
            collective_id=0, has_side_effects=True, vmem_limit_bytes=60 * 2**20
        ),
        name="migrate",
    )(freq_index, owner, wavefield, velocity[0], *tables())
    return hand_over(image, field)


def solution(mesh):
    return jax.shard_map(
        shards,
        mesh=mesh,
        in_specs=(P("freq", None, "space", None), P("freq", "space", None), P("freq"), P()),
        out_specs=(P(None, "space", "freq"), P("freq", None, "space", None)),
        check_vma=False,
    )
```

```python
import functools
import math

import jax
import jax.numpy as jnp
import ml_dtypes
import numpy as np
from jax import lax
from jax.experimental import pallas as pl
from jax.experimental.pallas import tpu as pltpu
from jax.sharding import PartitionSpec as P

NX, NY = 4096, 2048
SPACE, FREQ = 32, 8
ROWS = NY // SPACE
LANES = 128
TILES = NX // LANES
YA = NY // LANES
CHUNK = 32
CHUNKS = ROWS // CHUNK
BAND = NX // FREQ
PIECE = ROWS // FREQ
AHEAD, BEHIND, WINDOW = 32, 32, 32

cell_spacing = 25.0
layer_thickness = 10.0
base_speed = 1500.0
lowest_hertz = 5.0
hertz_step = 0.9
MESH = pl.DeviceIdType.MESH
f32 = jnp.float32
bf16 = jnp.bfloat16


def times_root(value, power, length, sign):
    re, im = value
    power = power % length
    quarter = 4 * power
    if quarter % length == 0:
        turn = quarter // length
        if sign < 0:
            turn = (4 - turn) % 4
        return [(re, im), (-im, re), (-re, -im), (im, -re)][turn]
    angle = sign * 2 * math.pi * power / length
    c, s = math.cos(angle), math.sin(angle)
    if (8 * power) % length == 0:
        h = math.sqrt(0.5)
        cs, ss = math.copysign(1, c), math.copysign(1, s)
        p, q = re * h, im * h
        real = (p if cs > 0 else -p) + (-q if ss > 0 else q)
        imag = (p if ss > 0 else -p) + (q if cs > 0 else -q)
        return (real, imag)
    return (re * c - im * s, re * s + im * c)


def add(a, b):
    return (a[0] + b[0], a[1] + b[1])


def sub(a, b):
    return (a[0] - b[0], a[1] - b[1])


def small_dft(values, sign):
    n = len(values)
    if n == 1:
        return values
    if n == 2:
        return [add(values[0], values[1]), sub(values[0], values[1])]
    m = n // 4
    parts = [small_dft(values[r::4], sign) for r in range(4)]
    out = [None] * n
    for k in range(m):
        a = parts[0][k]
        b, c, d = (times_root(parts[r][k], r * k, n, sign) for r in (1, 2, 3))
        s0, s1 = add(a, c), sub(a, c)
        s2, s3 = add(b, d), times_root(sub(b, d), 1, 4, sign)
        out[k], out[k + m] = add(s0, s2), add(s1, s3)
        out[k + 2 * m], out[k + 3 * m] = sub(s0, s2), sub(s1, s3)
    return out


def sin_cos(t):
    n = jnp.floor(t * (2 / math.pi) + 0.5)
    r = (t - n * 1.5703125) - n * 4.83826794896e-4
    z = r * r
    s = r + r * z * (-1.6666654611e-1 + z * (8.3321608736e-3 + z * -1.9515295891e-4))
    c = 1.0 - 0.5 * z + z * z * (4.166664568298827e-2 + z * (-1.388731625493765e-3 + z * 2.443315711809948e-5))
    half = n * 0.5
    odd = half != jnp.floor(half)
    quad = n - 4.0 * jnp.floor(n * 0.25)
    sine = jnp.where(odd, c, s)
    cosine = jnp.where(odd, s, c)
    sine = jnp.where(quad >= 2.0, -sine, sine)
    cosine = jnp.where((quad == 1.0) | (quad == 2.0), -cosine, cosine)
    return sine, cosine


def split(value):
    high = value.astype(bf16)
    return high, (value - high.astype(f32)).astype(bf16)


def mul3(a, b):
    ah, al = a
    bh, bl = b
    dot = functools.partial(jnp.dot, preferred_element_type=f32)
    return dot(ah, bh) + (dot(al, bh) + dot(ah, bl))


def left_mul3(left_ref, b):
    bh, bl = b
    n = bh.shape[0]
    dot = functools.partial(jnp.dot, preferred_element_type=f32)
    both = dot(left_ref[...], bh)
    return both[:n] + (both[n:] + dot(left_ref[:n, :], bl))


def kernel(
    fidx_ref, owner_ref, wave_ref, vel_ref, txc_ref, txs_ref, rh_ref, rl_ref, lh_ref, ll_ref, rs_ref, ls_ref,
    image_ref, field_ref,
    rowbuf, sendx, sendy, recvy, recvx, relay, mid, hcos, hsin, tyc, tys,
    vrecv, vsel, vpart, vturn, slow, phc, phs, terms, imag, irecv, isum, iback, omega_out, omega_in,
    asend, arecv, aloc, rsend, rrecv, zsend, zrecv, rloc,
    vsend, vrcv, vloc, isend, ircv, iloc, tsend, trecv, tloc, gate, gsend, grecv, csend, psend,
):
    f = lax.axis_index("freq")
    me = lax.axis_index("space")
    x, zl = f // 2, f % 2
    zh, y, c = me // 8, (me // 2) % 4, me % 2
    z = zh * 2 + zl
    here = (x * 4 + y) * 2 + c

    def dev(dx, dy, dzh, dzl, dc):
        return (dx * 2 + dzl, (dzh * 4 + dy) * 2 + dc)

    def plane(j):
        px, py, pc = (x + j % 4) % 4, (y + j // 4 + j) % 4, (c + j // 16) % 2
        return dev(px, py, zh, zl, pc), (px * 4 + py) * 2 + pc

    def along_z(j):
        pz = (z + j) % 8
        return dev(x, y, pz // 2, pz % 2, c), pz

    other_core = dev(x, y, zh, zl, 1 - c)
    across = dev(zh, y, x, zl, c)
    across_odd = dev(zh, y, x, 1 - zl, c)

    barrier = pltpu.get_barrier_semaphore()

    def greet(device):
        pl.semaphore_signal(barrier, inc=1, device_id=device, device_id_type=MESH)

    @pl.loop(1, 32)
    def _(j):
        greet(plane(j)[0])

    @pl.loop(1, 8)
    def _(j):
        greet(along_z(j)[0])

    @pl.loop(1, 4)
    def _(j):
        greet(dev((x + j) % 4, y, zh, 1 - zl, c))

    greet(across_odd)

    @pl.when(x != zh)
    def _():
        greet(across)

    @pl.when(x == zh)
    def _():
        greet(across_odd)

    def remote(src, dst, send, recv, device):
        return pltpu.make_async_remote_copy(
            src_ref=src, dst_ref=dst, send_sem=send, recv_sem=recv, device_id=device, device_id_type=MESH
        )

    def chunk_rows(ch):
        return pl.ds(ch * CHUNK, CHUNK)

    def a2a_start(src, dst, ch, i):
        rows = chunk_rows(ch)

        @pl.loop(1, 32)
        def _(j):
            device, place = plane(j)
            remote(src.at[place, rows], dst.at[here, rows], asend.at[i, ch], arecv.at[i, ch], device).start()

        pltpu.make_async_copy(src.at[here, rows], dst.at[here, rows], aloc.at[i, ch]).start()

    def a2a_start_core(src, dst, ch, i, core):
        rows = chunk_rows(ch)

        @pl.loop(0, 16)
        def _(k):
            px, py = (x + k % 4) % 4, (y + k // 4 + k) % 4
            place = (px * 4 + py) * 2 + core

            @pl.when(place != here)
            def _():
                remote(
                    src.at[place, rows], dst.at[here, rows], csend.at[core, ch], arecv.at[i, ch],
                    dev(px, py, zh, zl, core),
                ).start()

            @pl.when(place == here)
            def _():
                pltpu.make_async_copy(src.at[here, rows], dst.at[here, rows], aloc.at[i, ch]).start()

    def a2a_core_sent(dst, ch, i, core):
        @pl.when(c == core)
        def _():
            part = dst.at[pl.ds(0, 15), chunk_rows(ch)]
            remote(part, part, csend.at[core, ch], arecv.at[i, ch], across_odd).wait_send()

        @pl.when(c != core)
        def _():
            part = dst.at[pl.ds(0, 16), chunk_rows(ch)]
            remote(part, part, csend.at[core, ch], arecv.at[i, ch], across_odd).wait_send()

    def a2a_all(dst, ch, i):
        part = dst.at[pl.ds(0, SPACE - 1), chunk_rows(ch)]
        return remote(part, part, asend.at[i, ch], arecv.at[i, ch], across_odd)

    def a2a_wait_recv(dst, ch, i):
        a2a_all(dst, ch, i).wait_recv()
        part = dst.at[here, chunk_rows(ch)]
        pltpu.make_async_copy(part, part, aloc.at[i, ch]).wait()

    def spread_send(src, q, sent=False):
        k, pc = q % 16, q // 16
        px, py = (x + k + zh) % 4, (y + k // 4 + k) % 4
        place, slot = (px * 4 + py) * 2 + pc, k * 2 + c

        @pl.when(place != here)
        def _():
            copy = remote(
                src.at[place], relay.at[0, slot], psend.at[q], rrecv.at[0, slot], dev(px, py, zh, zl, pc)
            )
            if sent:
                copy.wait_send()
            else:
                copy.start()

    def spread_relay(src, dst, r):
        k, pc = r // 2, r % 2
        px, py = (x + 64 - k - zh) % 4, (y + 64 - k // 4 - k) % 4
        place, slot = (px * 4 + py) * 2 + pc, (zh * 4 + py) * 2 + pc
        target = dev(x, y, px, 1 - zl, c)

        @pl.when(place == here)
        def _():
            remote(src.at[here], dst.at[slot], zsend.at[0], zrecv.at[0], target).start()

        @pl.when(place != here)
        def _():
            remote(relay.at[0, r], relay.at[0, r], rsend.at[0], rrecv.at[0, r], across_odd).wait_recv()
            remote(relay.at[0, r], dst.at[slot], zsend.at[0], zrecv.at[0], target).start()

    def spread(src, dst):
        ahead = AHEAD + (32 - AHEAD) * c

        @pl.loop(0, ahead)
        def _(q):
            @pl.when(q >= WINDOW)
            def _():
                spread_send(src, q - WINDOW, True)

            spread_send(src, q)

        @pl.when(c == 1)
        def _():
            @pl.loop(32 - WINDOW, 32)
            def _(q):
                spread_send(src, q, True)

            velocity_start()
            pl.semaphore_wait(gate.at[0], 1)

        @pl.loop(0, 32)
        def _(r):
            spread_relay(src, dst, r)

            @pl.when((c == 0) & (r == 12))
            def _():
                velocity_start()

            @pl.when(ahead + r < 32)
            def _():
                spread_send(src, ahead + r - WINDOW, True)
                spread_send(src, ahead + r)

        @pl.when(c == 0)
        def _():
            @pl.loop(32 - WINDOW, 32)
            def _(q):
                spread_send(src, q, True)

            pl.semaphore_signal(gate.at[0], inc=1, device_id=other_core, device_id_type=MESH)

    def collect_send(src, i):
        ch, j = i // 32, i % 32
        rows = pl.ds(pl.multiple_of(ch * CHUNK, CHUNK), CHUNK)
        pzh, py, pc = (zh + j + x) % 4, (y + j // 8) % 4, (c + (j // 4) % 2) % 2
        remote(
            src.at[(pzh * 4 + py) * 2 + pc, rows], relay.at[1, j, rows],
            zsend.at[1 + ch], rrecv.at[1 + ch, j], dev(x, y, pzh, 1 - zl, c),
        ).start()

    def collect_relay(dst, i):
        ch, j = i // 32, i % 32
        rows = pl.ds(pl.multiple_of(ch * CHUNK, CHUNK), CHUNK)
        px, py, pc = (zh + 64 - j - x) % 4, (y + j // 8) % 4, (c + (j // 4) % 2) % 2
        place = (px * 4 + py) * 2 + pc
        part = relay.at[1, j, rows]
        remote(part, part, zsend.at[1 + ch], rrecv.at[1 + ch, j], across_odd).wait_recv()

        @pl.when(place == here)
        def _():
            pltpu.make_async_copy(part, dst.at[here, rows], rloc.at[ch]).start()

        @pl.when(place != here)
        def _():
            remote(part, dst.at[here, rows], rsend.at[1 + ch], zrecv.at[1 + ch], dev(px, py, zh, zl, pc)).start()

    def collect(src, dst, low, high):
        @pl.loop(low, high)
        def _(i):
            collect_relay(dst, i)

            @pl.when(BEHIND + i < 32 * CHUNKS)
            def _():
                collect_send(src, BEHIND + i)

    def collect_all(dst, ch):
        part = dst.at[pl.ds(0, SPACE - 1), chunk_rows(ch)]
        return remote(part, part, rsend.at[1 + ch], zrecv.at[1 + ch], across_odd)

    def collect_wait_recv(dst, ch):
        collect_all(dst, ch).wait_recv()
        part = dst.at[here, chunk_rows(ch)]
        pltpu.make_async_copy(part, part, rloc.at[ch]).wait()

    def forward_x(re_ref, im_ref, dst, ch):
        @pl.loop(0, CHUNK // 8)
        def _(g):
            rows = pl.ds(pl.multiple_of(ch * CHUNK + g * 8, 8), 8)
            local = pl.ds(pl.multiple_of(g * 8, 8), 8)
            vals = [
                (re_ref[rows, a * LANES:(a + 1) * LANES], im_ref[rows, a * LANES:(a + 1) * LANES])
                for a in range(TILES)
            ]
            vals = small_dft(vals, -1)
            for k in range(TILES):
                re, im = vals[k]
                c, s = txc_ref[k:k + 1, :], txs_ref[k:k + 1, :]
                rowbuf[k, local, 0:LANES] = re * c + im * s
                rowbuf[k, local, LANES:] = im * c - re * s

        @pl.loop(0, TILES // 8)
        def _(g):
            some = pl.ds(g * 8, 8)
            block = rowbuf[some].reshape(8 * CHUNK, 2 * LANES)
            out = mul3(split(block), (rh_ref[...], rl_ref[...]))
            dst[some, pl.ds(ch * CHUNK, CHUNK), :] = out.reshape(8, CHUNK, 2 * LANES)

    def inverse_x(src, step, re_ref, im_ref, ch):
        @pl.loop(0, TILES // 8)
        def _(g):
            some = pl.ds(g * 8, 8)
            block = src[some, pl.ds(ch * CHUNK, CHUNK), :].reshape(8 * CHUNK, 2 * LANES)
            out = mul3(split(block), (lh_ref[...], ll_ref[...]))
            rowbuf[some] = out.reshape(8, CHUNK, 2 * LANES)

        @pl.loop(0, CHUNK // 8)
        def _(g):
            rows = pl.ds(pl.multiple_of(ch * CHUNK + g * 8, 8), 8)
            local = pl.ds(pl.multiple_of(g * 8, 8), 8)
            vals = []
            for k in range(TILES):
                re, im = rowbuf[k, local, 0:LANES], rowbuf[k, local, LANES:]
                c, s = txc_ref[k:k + 1, :], txs_ref[k:k + 1, :]
                vals.append((re * c - im * s, im * c + re * s))
            vals = small_dft(vals, 1)
            for a in range(TILES):
                re, im = vals[a]
                cols = slice(a * LANES, (a + 1) * LANES)
                c, s = phc[step, rows, cols], phs[step, rows, cols]
                re_ref[rows, cols] = re * c - im * s
                im_ref[rows, cols] = re * s + im * c

    def column_pass(src, dst, send):
        @pl.loop(0, LANES // 8)
        def _(t):
            half, sub_rows = t // 8, pl.ds(pl.multiple_of(t % 8 * 8, 8), 8)
            vals = [
                (src[2 * a + half, sub_rows, 0:LANES], src[2 * a + half, sub_rows, LANES:]) for a in range(YA)
            ]
            vals = small_dft(vals, -1)
            re_rows = pl.ds(pl.multiple_of(t * 8, 8), 8)
            im_rows = pl.ds(pl.multiple_of(LANES + t * 8, 8), 8)
            for k in range(YA):
                re, im = vals[k]
                cols = slice(k % 2 * LANES, k % 2 * LANES + LANES)
                c, s = tyc[k // 2, re_rows, cols], tys[k // 2, re_rows, cols]
                mid[k // 2, re_rows, cols] = re * c + im * s
                mid[k // 2, im_rows, cols] = im * c - re * s

        @pl.loop(0, YA // 2)
        def _(k):
            spec = left_mul3(ls_ref, split(mid[k]))
            re, im = spec[:LANES], spec[LANES:]
            c, s = hcos[k], hsin[k]
            spec = jnp.concatenate([re * c - im * s, re * s + im * c], axis=0)
            mid[k] = left_mul3(rs_ref, split(spec))

        for ch in range(CHUNKS):
            @pl.loop(0, CHUNK // 4)
            def _(q):
                half, tile = q % 2, ch * (CHUNK // 8) + q // 2
                t = half * 8 + tile
                re_rows = pl.ds(pl.multiple_of(t * 8, 8), 8)
                im_rows = pl.ds(pl.multiple_of(LANES + t * 8, 8), 8)
                vals = []
                for k in range(YA):
                    cols = slice(k % 2 * LANES, k % 2 * LANES + LANES)
                    re, im = mid[k // 2, re_rows, cols], mid[k // 2, im_rows, cols]
                    c, s = tyc[k // 2, re_rows, cols], tys[k // 2, re_rows, cols]
                    vals.append((re * c - im * s, im * c + re * s))
                vals = small_dft(vals, 1)
                out_rows = pl.ds(pl.multiple_of(tile * 8, 8), 8)
                for a in range(YA):
                    dst[2 * a + half, out_rows, 0:LANES] = vals[a][0]
                    dst[2 * a + half, out_rows, LANES:] = vals[a][1]
            send(ch)

    def make_twiddles():
        kb = lax.broadcasted_iota(jnp.int32, (LANES, LANES), 0)

        @pl.loop(0, YA // 2)
        def _(k):
            for part in range(2):
                cols = slice(part * LANES, (part + 1) * LANES)
                sine, cosine = sin_cos(((2 * k + part) * kb).astype(f32) * (2 * math.pi / NY))
                tyc[k, :, cols] = cosine
                tys[k, :, cols] = sine

    def make_tables(omega):
        kb = lax.broadcasted_iota(jnp.int32, (LANES, LANES), 0)
        lane = lax.broadcasted_iota(jnp.int32, (LANES, LANES), 1)
        jx = here + TILES * lane
        kx = jnp.where(jx < NX // 2, jx, jx - NX).astype(f32) * (2 * math.pi / (NX * cell_spacing))

        @pl.loop(0, YA // 2)
        def _(k):
            for part in range(2):
                ka = 2 * k + part
                cols = slice(part * LANES, (part + 1) * LANES)
                jy = ka + YA * kb
                ky = jnp.where(jy < NY // 2, jy, jy - NY).astype(f32) * (2 * math.pi / (NY * cell_spacing))
                vertical = (omega / base_speed) ** 2 - (ky * ky + kx * kx)
                root = layer_thickness * jnp.sqrt(jnp.abs(vertical))
                damping = jnp.exp(jnp.where(vertical < 0.0, -root, 0.0)) * (1.0 / (NX * NY))
                sine, cosine = sin_cos(jnp.where(vertical > 0.0, root, 0.0))
                hcos[k, :, cols] = damping * cosine
                hsin[k, :, cols] = damping * sine

    def make_phase(step, omega):
        @pl.loop(0, ROWS // 8)
        def _(g):
            rows = pl.ds(pl.multiple_of(g * 8, 8), 8)
            for q in range(4):
                cols = slice(q * NX // 4, (q + 1) * NX // 4)
                shift = (omega * layer_thickness) * slow[step, rows, cols]
                sine, cosine = sin_cos(shift)
                phc[step, rows, cols] = cosine
                phs[step, rows, cols] = sine

    quarter = pl.ds(pl.multiple_of(x * 2 * PIECE, 2 * PIECE), 2 * PIECE)

    def velocity_start():
        @pl.loop(1, 4)
        def _(j):
            px = (x + j) % 4
            rows = pl.ds(pl.multiple_of(px * 2 * PIECE, 2 * PIECE), 2 * PIECE)
            remote(vel_ref.at[rows], vrecv.at[x], vsend.at[0], vrcv.at[0], dev(px, y, zh, zl, c)).start()

        pltpu.make_async_copy(vel_ref.at[quarter], vrecv.at[x], vloc.at[0]).start()

    def velocity_all():
        part = vrecv.at[pl.ds(0, 3)]
        return remote(part, part, vsend.at[0], vrcv.at[0], across_odd)

    partner = dev(x, y, zh, 1 - zl, c)
    own_half = pl.ds(pl.multiple_of(zl * PIECE, PIECE), PIECE)
    other_half = pl.ds(pl.multiple_of((1 - zl) * PIECE, PIECE), PIECE)
    pair0 = remote(vsel.at[0, other_half], vpart.at[0, pl.ds(0, PIECE)], vsend.at[1], vrcv.at[1], partner)
    pair1 = remote(vsel.at[1], vpart.at[1], vsend.at[2], vrcv.at[2], partner)
    turn = remote(vsel.at[2, pl.ds(0, PIECE)], vturn, vsend.at[3], vrcv.at[3], across)
    turn_here = pltpu.make_async_copy(vsel.at[2, pl.ds(0, PIECE)], vturn, vloc.at[1])

    def velocity_select():
        velocity_all().wait_recv()
        pltpu.make_async_copy(vel_ref.at[quarter], vrecv.at[x], vloc.at[0]).wait()
        for step in range(2):
            chosen = owner_ref[step]
            piece = 1.0 / vrecv[chosen // 2] - 1.0 / base_speed
            vsel[step] = jnp.where(chosen % 2 == zl, piece, 0.0)
        pair0.start()

    def velocity_turn():
        pair0.wait_recv()
        vsel[2, 0:PIECE] = vsel[0, own_half] + vpart[0, 0:PIECE]

        @pl.when(x != zh)
        def _():
            turn.start()

        @pl.when(x == zh)
        def _():
            turn_here.start()

    def velocity_spread():
        @pl.when(x != zh)
        def _():
            turn.wait_recv()

        @pl.when(x == zh)
        def _():
            turn_here.wait()

        velocity_along_z()

    eighth = pl.ds(pl.multiple_of(z * PIECE, PIECE), PIECE)

    def ring_copy(k):
        offset = (2, -2, 1, -1, 1, -1, 2, -2)[k]
        source = (0, 0, 0, 0, -2, 2, -2, 2)[k]
        cols = (slice(0, NX // 2) if k == 6 else slice(NX // 2, NX)) if k >= 6 else slice(0, NX)
        rows = pl.ds(pl.multiple_of((z + 8 + source) % 8 * PIECE, PIECE), PIECE)
        part = slow.at[0, rows, cols]
        return remote(part, part, gsend.at[k], grecv.at[k], along_z((8 + offset) % 8)[0])

    def velocity_along_z():
        slow[0, eighth] = vturn[...]
        for k in range(4):
            ring_copy(k).start()

    def velocity_forward():
        for k in range(2):
            ring_copy(k).wait_recv()
            ring_copy(4 + k).start()
            ring_copy(6 + k).start()
        for k in range(2, 8):
            ring_copy(k).wait_recv()

    def velocity_along_x():
        pair1.wait_recv()
        piece = vsel[1] + vpart[1]
        vsel[3] = piece
        slow[1, quarter] = piece

        @pl.loop(1, 4)
        def _(j):
            remote(vsel.at[3], slow.at[1, quarter], vsend.at[5], vrcv.at[5], dev((x + j) % 4, y, zh, zl, c)).start()

    def along_x_all():
        part = slow.at[1, pl.ds(0, 6 * PIECE)]
        return remote(part, part, vsend.at[5], vrcv.at[5], across_odd)

    def image_start(step, ch):
        rows = chunk_rows(ch)
        mine = z if step == 0 else f

        @pl.loop(1, 8)
        def _(j):
            if step == 0:
                device, p = along_z(j)
            else:
                p = (f + j) % 8
                device = (p, me)
            cols = pl.ds(pl.multiple_of(p * BAND, BAND), BAND)
            remote(
                terms.at[step, rows, cols], irecv.at[step, mine, rows],
                isend.at[step, ch], ircv.at[step, ch], device,
            ).start()

        cols = pl.ds(pl.multiple_of(mine * BAND, BAND), BAND)
        pltpu.make_async_copy(terms.at[step, rows, cols], irecv.at[step, mine, rows], iloc.at[step, ch]).start()

    def image_all(step, ch):
        part = irecv.at[step, pl.ds(0, FREQ - 1), chunk_rows(ch)]
        return remote(part, part, isend.at[step, ch], ircv.at[step, ch], across_odd)

    def image_sum(step, ch):
        rows = chunk_rows(ch)
        image_all(step, ch).wait_recv()
        part = irecv.at[step, 0, rows]
        pltpu.make_async_copy(part, part, iloc.at[step, ch]).wait()
        total = irecv[step, 0, rows, :]
        for j in range(1, FREQ):
            total = total + irecv[step, j, rows, :]
        return rows, total

    back = remote(isum, iback, tsend.at[0], trecv.at[0], across)
    back_here = pltpu.make_async_copy(isum, iback, tloc.at[0])

    omega = 2 * math.pi * (lowest_hertz + hertz_step * fidx_ref[0].astype(f32))
    omega_out[...] = jnp.full((8, LANES), omega, f32)
    omega_turn = remote(omega_out, omega_in, tsend.at[1], trecv.at[1], across_odd)
    for ch in range(CHUNKS):
        forward_x(wave_ref.at[0, 0], wave_ref.at[0, 1], sendx.at[0], ch)
    make_twiddles()
    pl.semaphore_wait(barrier, 31 + 7 + 3 + 1 + 1)
    omega_turn.start()
    spread(sendx.at[0], recvy.at[0])
    omega_turn.wait_recv()
    omega_col = omega_in[0:1, :]
    velocity_select()
    make_tables(omega_col)
    recvy_all = remote(recvy.at[0], recvy.at[0], zsend.at[0], zrecv.at[0], across_odd)

    @pl.when(c == 1)
    def _():
        velocity_turn()

    recvy_all.wait_recv()
    pl.semaphore_signal(gate.at[1], inc=1, device_id=other_core, device_id_type=MESH)

    @pl.when(c == 1)
    def _():
        pl.semaphore_wait(gate.at[1], 1)
        velocity_spread()

    column_pass(recvy.at[0], sendy.at[0], lambda ch: a2a_start(sendy.at[0], recvx.at[0], ch, 0))


    @pl.when(c == 0)
    def _():
        velocity_turn()
        pl.semaphore_wait(gate.at[1], 1)
        velocity_spread()

    velocity_forward()
    make_phase(0, omega_in[0:1, 0:1])
    for ch in range(CHUNKS):
        a2a_wait_recv(recvx.at[0], ch, 0)
        inverse_x(recvx.at[0], 0, terms.at[0], imag, ch)
        forward_x(terms.at[0], imag, sendx.at[1], ch)
        a2a_start_core(sendx.at[1], recvy.at[1], ch, 1, 0)
        image_start(0, ch)
    for ch in range(CHUNKS):
        a2a_core_sent(sendx.at[1], ch, 1, 0)
        a2a_start_core(sendx.at[1], recvy.at[1], ch, 1, 1)
    pair1.start()
    for ch in range(CHUNKS):
        a2a_wait_recv(recvy.at[1], ch, 1)

    def collect_first(ch):
        if ch == 0:
            @pl.loop(0, BEHIND)
            def _(i):
                collect_send(sendy.at[1], i)

    column_pass(recvy.at[1], sendy.at[1], collect_first)
    velocity_along_x()
    for ch in range(CHUNKS):
        rows, total = image_sum(0, ch)
        isum[rows, :] = total

    @pl.when(x != zh)
    def _():
        back.start()

    @pl.when(x == zh)
    def _():
        back_here.start()

    def finish(ch):
        collect_wait_recv(recvx.at[1], ch)
        inverse_x(recvx.at[1], 1, terms.at[1], field_ref.at[0, 1], ch)
        image_start(1, ch)
        rows = chunk_rows(ch)
        field_ref[0, 0, rows, :] = terms[1, rows, :]

    collect(sendy.at[1], recvx.at[1], 0, 32)
    along_x_all().wait_recv()
    make_phase(1, omega)
    for ch in range(1, CHUNKS):
        collect(sendy.at[1], recvx.at[1], 32 * ch, 32 * ch + 16)
        finish(ch - 1)
        collect(sendy.at[1], recvx.at[1], 32 * ch + 16, 32 * ch + 32)
    finish(CHUNKS - 1)

    @pl.when(x != zh)
    def _():
        back.wait()
        turn.wait_send()

    @pl.when(x == zh)
    def _():
        back_here.wait()

    image_ref[0] = iback[...]
    for ch in range(CHUNKS):
        rows, total = image_sum(1, ch)
        image_ref[1, rows, :] = total

    omega_turn.wait_send()
    recvy_all.wait_send()
    velocity_all().wait_send()
    pair0.wait_send()
    pair1.wait_send()
    for k in range(8):
        ring_copy(k).wait_send()
    along_x_all().wait_send()
    for ch in range(CHUNKS):
        part = relay.at[1, :, chunk_rows(ch)]
        remote(part, part, zsend.at[1 + ch], rrecv.at[1 + ch, 0], across_odd).wait_send()
        collect_all(recvx.at[1], ch).wait_send()
        a2a_all(recvx.at[0], ch, 0).wait_send()
        a2a_core_sent(sendx.at[1], ch, 1, 1)
        for step in range(2):
            image_all(step, ch).wait_send()


def tables():
    n = np.arange(LANES)
    angle = 2 * np.pi * ((n[:, None] * n[None, :]) % LANES) / LANES
    c, s = np.cos(angle), np.sin(angle)
    right = np.block([[c, -s], [s, c]])
    out = []
    for m in (right, right.T):
        high = m.astype(ml_dtypes.bfloat16)
        out += [high, (m - high.astype(np.float64)).astype(ml_dtypes.bfloat16)]
    out += [np.concatenate(out[:2]), np.concatenate(out[2:4])]
    tx = 2 * np.pi * ((np.arange(TILES)[:, None] * n[None, :]) % NX) / NX
    return [np.cos(tx).astype(np.float32), np.sin(tx).astype(np.float32)] + out


def hand_kernel(image_in, field_in, image_out, field_out):
    image_out[...] = image_in[...]
    field_out[...] = field_in[...]


def hand_over(image, field):
    specs = (
        pl.BlockSpec((2, ROWS // 4, BAND), lambda i: (0, i, 0)),
        pl.BlockSpec((1, 2, ROWS // 4, NX), lambda i: (0, 0, i, 0)),
    )
    return pl.pallas_call(
        hand_kernel,
        grid=(4,),
        out_shape=(
            jax.ShapeDtypeStruct(image.shape, f32),
            jax.ShapeDtypeStruct(field.shape, f32),
        ),
        in_specs=specs,
        out_specs=specs,
        name="hand_over",
    )(image, field)


def shards(wavefield, velocity, freq_index, owner):
    vmem = pl.BlockSpec(memory_space=pltpu.VMEM)
    smem = pl.BlockSpec(memory_space=pltpu.SMEM)
    dma = pltpu.SemaphoreType.DMA
    big = (SPACE, ROWS, 2 * LANES)
    image, field = pl.pallas_call(
        kernel,
        out_shape=(
            jax.ShapeDtypeStruct((2, ROWS, BAND), f32),
            jax.ShapeDtypeStruct((1, 2, ROWS, NX), f32),
        ),
        in_specs=[smem, smem] + [vmem] * 10,
        out_specs=(vmem, vmem),
        scratch_shapes=[
            pltpu.VMEM((TILES, CHUNK, 2 * LANES), f32),
            pltpu.VMEM((2,) + big, f32),
            pltpu.VMEM((2,) + big, f32),
            pltpu.VMEM((2,) + big, f32),
            pltpu.VMEM((2,) + big, f32),
            pltpu.VMEM((2,) + big, f32),
            pltpu.VMEM((YA // 2, 2 * LANES, 2 * LANES), f32),
            pltpu.VMEM((YA // 2, LANES, 2 * LANES), f32),
            pltpu.VMEM((YA // 2, LANES, 2 * LANES), f32),
            pltpu.VMEM((YA // 2, LANES, 2 * LANES), f32),
            pltpu.VMEM((YA // 2, LANES, 2 * LANES), f32),
            pltpu.VMEM((4, 2 * PIECE, NX), f32),
            pltpu.VMEM((4, 2 * PIECE, NX), f32),
            pltpu.VMEM((2, 2 * PIECE, NX), f32),
            pltpu.VMEM((PIECE, NX), f32),
            pltpu.VMEM((2, ROWS, NX), f32),
            pltpu.VMEM((2, ROWS, NX), f32),
            pltpu.VMEM((2, ROWS, NX), f32),
            pltpu.VMEM((2, ROWS, NX), f32),
            pltpu.VMEM((ROWS, NX), f32),
            pltpu.VMEM((2, FREQ, ROWS, BAND), f32),
            pltpu.VMEM((ROWS, BAND), f32),
            pltpu.VMEM((ROWS, BAND), f32),
            pltpu.VMEM((8, LANES), f32),
            pltpu.VMEM((8, LANES), f32),
            dma((2, CHUNKS)), dma((2, CHUNKS)), dma((2, CHUNKS)),
            dma((1 + CHUNKS,)), dma((1 + CHUNKS, 32)), dma((1 + CHUNKS,)), dma((1 + CHUNKS,)), dma((CHUNKS,)),
            dma((6,)), dma((6,)), dma((2,)),
            dma((2, CHUNKS)), dma((2, CHUNKS)), dma((2, CHUNKS)),
            dma((2,)), dma((2,)), dma((1,)), pltpu.SemaphoreType.REGULAR((2,)), dma((8,)), dma((8,)), dma((2, CHUNKS)), dma((32,)),
        ],
        compiler_params=pltpu.CompilerParams(
            collective_id=0, has_side_effects=True, vmem_limit_bytes=60 * 2**20
        ),
        name="migrate",
    )(freq_index, owner, wavefield, velocity[0], *tables())
    return hand_over(image, field)


def solution(mesh):
    return jax.shard_map(
        shards,
        mesh=mesh,
        in_specs=(P("freq", None, "space", None), P("freq", "space", None), P("freq"), P()),
        out_specs=(P(None, "space", "freq"), P("freq", None, "space", None)),
        check_vma=False,
    )
```
